512 devices in a mesh: dp: 32 (over y, z_lo, core), expert: 16 (over z_hi, x).
Axes of the slice: x: 4, y: 4, z: 16 (z_hi: 4, z_lo: 4; z = z_hi * 4 + z_lo), core: 2. Of those that a mesh axis runs over, the one named last changes fastest.
Arguments:
- tokens: bfloat16 [2048, 4096], P('expert', 'dp'), may hold values from -6 to 6
- out_grad: bfloat16 [2048, 4096], P('expert', 'dp'), may hold values from -0.29882812 to 0.29882812
- expert_ids: int32 [2048, 2], P('expert'), may hold values from 0 to 15, all different within a row; in each aligned block of 128 rows (0 to 127, 128 to 255, ...) at most 30 rows name the same one
- gate_weights: float32 [2048, 2], P('expert'), may hold values from 0.1 to 1
- w_in: bfloat16 [16, 4096, 4096], P('expert', None, 'dp'), may hold values from -0.09375 to 0.09375
- w_out: bfloat16 [16, 4096, 4096], P('expert', 'dp'), may hold values from -0.09375 to 0.09375
Outputs:
- tokens_grad: bfloat16 [2048, 4096], P('expert', 'dp')
- w_in_grad: bfloat16 [16, 4096, 4096], P('expert', None, 'dp')
- w_out_grad: bfloat16 [16, 4096, 4096], P('expert', 'dp')
The draws below stay inside these ranges and needn't reach their ends.
Inputs may be any that keep to these rules, and one draw needn't show every extreme that they name: `expert_ids`: in each row the two ids differ. In the rows of one block no expert is named by more than 30 rows, and in some blocks one expert is named by exactly 30.
All inputs are finite; a program needn't handle non-finite values.
Results may differ from the reference program's by a relative error of at most 0.03.
Values may be sent and summed in bfloat16 or wider, within the bound.
No kernel may reach another device: no remote copies, remote signals or barrier semaphores. Data moves between devices by JAX's collectives and lax.ppermute only.
A program may use at most 64 MiB of HBM per device.

```python
import math
import jax
import jax.numpy as jnp
import numpy as np
from jax import lax

D = 4096
HID = 4096
TOK_DEV = 128
EXPERTS = 16
TOKENS = 2048
CAP = 20
MOST = 30
N_DP = 32


def steps_of(key, dims, split, least, largest):
    def one(dim, blocks):
        draws = jax.random.uniform(jax.random.fold_in(jax.random.fold_in(key, 6), dim), (blocks,), jnp.float32, least / len(split), largest / len(split))
        return jnp.repeat(jnp.exp(draws), dims[dim] // blocks).reshape((-1,) + (1,) * (len(dims) - dim - 1))

    factor_of = one(*split[0])
    for cut in split[1:]:
        factor_of = factor_of * one(*cut)
    return factor_of


def assign_block(own_key, own, number, rows, number_of, top, limit, lean):
    order = jax.random.permutation(own_key, number_of)
    crowded, ordinary = portions_of(number_of, rows * top, limit, lean, True), portions_of(number_of, rows * top, limit, lean, False)
    places = jnp.arange(number_of)

    def named(sizes, offset_by):
        used = int((sizes > 0).sum())
        fixed = max(1, used // 4)
        moved = fixed + (places - fixed + offset_by * (used - fixed)) % max(1, number_of - fixed)
        return jnp.zeros((number_of,), jnp.int32).at[order[jnp.where(places < fixed, places, moved)]].set(jnp.asarray(sizes, jnp.int32))

    sizes = jnp.where(number % 4 == 0, named(crowded, number // 4), named(ordinary, number - number // 4 - 1))
    mixed = jax.random.permutation(jax.random.fold_in(own, 3), number_of)
    donor, receiver = mixed[0:number_of // 2 * 2:2], mixed[1:number_of // 2 * 2:2]
    room = jnp.minimum(sizes[donor] - 1, limit - sizes[receiver]) // 2
    room = jnp.where((donor == order[0]) | (receiver == order[0]) | (sizes[receiver] == 0), 0, jnp.maximum(room, 0))
    moved = jax.random.randint(jax.random.fold_in(own, 4), (number_of // 2,), 0, 1 << 20) % (room + 1)
    sizes = sizes.at[donor].add(-moved).at[receiver].add(moved)
    items = jnp.searchsorted(jnp.cumsum(sizes), jnp.arange(rows * top), side="right").astype(jnp.int32)
    grid = items.reshape(top, rows).T
    grid = grid[jax.random.permutation(jax.random.fold_in(own, 1), rows)]
    offset_by = jax.random.randint(jax.random.fold_in(own, 2), (rows, 1), 0, top)
    return jnp.take_along_axis(grid, (jnp.arange(top)[None, :] + offset_by) % top, axis=1)


def portions_of(amount, total, most, skew, full):
    loads = [(1 << 20) // math.isqrt(grade ** skew) + 1 for grade in range(1, amount + 1)]
    largest = most if full else min(most, max(-(-total // amount), total * loads[0] // sum(loads)))
    least = 1 if total - largest >= amount - 1 else 0
    holding, surplus = [largest] + [least] * (amount - 1), total - largest - least * (amount - 1)
    while surplus > 0:
        movable = [i for i in range(1, amount) if holding[i] < largest] or [i for i in range(1, amount) if holding[i] < most]
        pool, remaining = sum([loads[i] for i in movable]), surplus
        for i in movable:
            extra = min(most - holding[i], max(1, remaining * loads[i] // pool), surplus)
            holding[i] = holding[i] + extra
            surplus = surplus - extra
    return np.array(holding)


def noise(key, shape, scale, bound, shards=(), kind=jnp.bfloat16):
    drawn = jax.random.normal(key, shape, jnp.float32) * scale
    if len(shards) > 0:
        drawn = steps_of(key, shape, shards, -0.22, 0.18) * drawn
    return jnp.clip(drawn, min=-bound, max=bound).astype(kind)


def setup_inputs(seed: int = 0) -> dict:
    keys = jax.random.split(jax.random.key(seed), 7)
    tokens = noise(keys[0], (TOKENS, D), 1.0, 6.0, ((0, 16), (1, 32)))
    out_grad = noise(keys[1], (TOKENS, D), 0.05, 0.29882812, ((0, 16), (1, 32)))
    expert_ids_keys = jax.random.split(jax.random.fold_in(keys[2], 1), TOKENS // TOK_DEV)
    expert_ids_turns = jax.random.permutation(jax.random.fold_in(keys[2], 3), TOKENS // TOK_DEV)
    expert_ids = jax.vmap(lambda own, number: assign_block(jax.random.fold_in(keys[2], 2), own, number, TOK_DEV, EXPERTS, 2, MOST, 2))(expert_ids_keys, expert_ids_turns).reshape((TOKENS, 2))
    gate_weights = jnp.clip(0.1 + 0.9 * jax.random.uniform(keys[3], (TOKENS, 2), jnp.float32) ** steps_of(keys[3], (TOKENS, 2), ((0, 16),), -0.2, 0.2), 0.1, 1.0)
    w_in = noise(keys[4], (EXPERTS, D, HID), D ** -0.5, 0.09375, ((0, 16), (2, 32)))
    w_out = noise(keys[5], (EXPERTS, HID, D), HID ** -0.5, 0.09375, ((0, 16), (1, 32)))
    return {"tokens": tokens, "out_grad": out_grad, "expert_ids": expert_ids, "gate_weights": gate_weights, "w_in": w_in, "w_out": w_out}


def activate(value):
    return jax.nn.gelu(value, approximate=True)

def reference(tokens, out_grad, expert_ids, gate_weights, w_in, w_out):
    nblocks = TOKENS // TOK_DEV
    width = tokens.shape[1]
    routed = expert_ids.reshape(nblocks, TOK_DEV, 2)
    gating = gate_weights.reshape(nblocks, TOK_DEV, 2)
    onehot = (routed[..., None] == jnp.arange(EXPERTS, dtype=jnp.int32)).astype(jnp.int32)
    counts = onehot.sum(2)
    prior = jnp.cumsum(counts, axis=1) - counts
    slot = lax.optimization_barrier(jnp.sum(onehot * prior[:, :, None, :], axis=-1)).astype(jnp.int32)
    kept = slot < CAP
    column = jnp.where(kept, slot, CAP).astype(jnp.int32)
    block_index = jnp.broadcast_to(jnp.arange(nblocks, dtype=jnp.int32)[:, None, None], routed.shape)
    token_index = jnp.broadcast_to(jnp.arange(TOK_DEV, dtype=jnp.int32)[None, :, None], routed.shape)
    owner = jnp.full((nblocks, EXPERTS, CAP + 1), TOK_DEV, jnp.int32).at[block_index, routed, column].set(token_index)
    weight_table = jnp.zeros((nblocks, EXPERTS, CAP + 1), jnp.float32).at[block_index, routed, column].set(gating)
    token_blocks = tokens.reshape(nblocks, TOK_DEV, width)
    grad_blocks = out_grad.reshape(nblocks, TOK_DEV, width)
    share = HID // N_DP

    def one_expert(which):
        index = lax.dynamic_index_in_dim(owner, which, 1, keepdims=False)[:, :CAP]
        scale = lax.dynamic_index_in_dim(weight_table, which, 1, keepdims=False)[:, :CAP]
        valid = index < TOK_DEV
        safe = jnp.minimum(index, TOK_DEV - 1).astype(jnp.int32)
        picked = jnp.take_along_axis(token_blocks, safe[:, :, None], axis=1)
        picked = jnp.where(valid[:, :, None], picked, jnp.zeros((), jnp.bfloat16))
        grads = jnp.take_along_axis(grad_blocks, safe[:, :, None], axis=1).astype(jnp.float32)
        expert_dy = (grads * scale[:, :, None]).astype(jnp.bfloat16)
        rows_in = picked.reshape(-1, width)
        rows_dy = expert_dy.reshape(-1, width)
        weight_in = lax.dynamic_index_in_dim(w_in, which, 0, keepdims=False)
        weight_out = lax.dynamic_index_in_dim(w_out, which, 0, keepdims=False)
        pre = jnp.dot(rows_in, weight_in, preferred_element_type=jnp.float32)
        act_grad = jnp.dot(rows_dy, weight_out.T, preferred_element_type=jnp.float32)
        act, pullback = jax.vjp(activate, pre)
        pre_grad = pullback(act_grad)[0].astype(jnp.bfloat16)
        act_low = act.astype(jnp.bfloat16)
        grad_in = jnp.dot(rows_in.T, pre_grad, preferred_element_type=jnp.float32).astype(jnp.bfloat16)
        grad_out = jnp.dot(act_low.T, rows_dy, preferred_element_type=jnp.float32).astype(jnp.bfloat16)
        split_grad = pre_grad.reshape(-1, N_DP, share).astype(jnp.float32)
        split_weight = weight_in.reshape(width, N_DP, share).astype(jnp.float32)
        parts = jnp.einsum('rih,dih->ird', split_grad, split_weight).astype(jnp.bfloat16)
        parts = lax.optimization_barrier(parts)
        rows_back = lax.optimization_barrier(jnp.sum(parts.astype(jnp.float32), axis=0)).astype(jnp.bfloat16)
        return (rows_back.reshape(nblocks, CAP, width), grad_in, grad_out)
    back_rows, w_in_grad, w_out_grad = lax.map(one_expert, jnp.arange(EXPERTS, dtype=jnp.int32))
    total = jnp.zeros((nblocks, TOK_DEV, width), jnp.float32)
    for pick in range(2):
        chosen = routed[:, :, pick]
        place = jnp.where(kept[:, :, pick], slot[:, :, pick], 0).astype(jnp.int32)
        values = back_rows[chosen, block_index[:, :, pick], place].astype(jnp.float32)
        total = total + jnp.where(kept[:, :, pick][:, :, None], values, 0.0)
    tokens_grad = total.astype(jnp.bfloat16).reshape(TOKENS, width)
    return (tokens_grad, w_in_grad, w_out_grad)
```

```python
import jax
import jax.numpy as jnp
from jax import lax
from jax.experimental import pallas as pl
from jax.experimental.pallas import tpu as pltpu
from jax.sharding import Mesh, PartitionSpec as P

NY, NZ, NC, NH, NX = 4, 4, 2, 4, 4
EXPERTS = NH * NX
TOK = 128
CAP = 20
MSG = 2 * CAP
COLS = 128
HID = 128
ROWS = EXPERTS * MSG
KEPT = EXPERTS * CAP
BF16 = jnp.bfloat16
F32 = jnp.float32
VMEM = pltpu.CompilerParams(vmem_limit_bytes=56 * 1024 * 1024)
CONTRACT_LAST = (((1,), (1,)), ((), ()))
CONTRACT_FIRST = (((0,), (0,)), ((), ()))


def slot_table(ids, rows_each, slot_of):
    experts = lax.broadcasted_iota(jnp.int32, (EXPERTS, TOK), 0)
    named = (experts == ids[0:1, :]) | (experts == ids[1:2, :])
    earlier = lax.broadcasted_iota(jnp.int32, (TOK, TOK), 0) < lax.broadcasted_iota(jnp.int32, (TOK, TOK), 1)
    prior = jnp.dot(named.astype(BF16), earlier.astype(BF16), preferred_element_type=F32)
    place = jnp.where(named, prior, -1.0).astype(BF16)
    shape = (EXPERTS, rows_each, TOK)
    expert = lax.broadcasted_iota(jnp.int32, shape, 0).reshape(EXPERTS * rows_each, TOK)
    row = lax.broadcasted_iota(jnp.int32, shape, 1).reshape(EXPERTS * rows_each, TOK)
    spread = (expert[:, :EXPERTS] == lax.broadcasted_iota(jnp.int32, (EXPERTS * rows_each, EXPERTS), 1)).astype(BF16)
    place_of_row = jnp.dot(spread, place, preferred_element_type=F32)
    return place_of_row == slot_of(row).astype(F32), expert, row


def dispatch_kernel(ids_ref, gate_ref, tok_ref, dy_ref, out_ref):
    ids = ids_ref[...]
    table, expert, row = slot_table(ids, MSG, lambda q: jnp.where(q >= CAP, q - CAP, q))
    gate = jnp.where(expert == ids[0:1, :], gate_ref[0:1, :], gate_ref[1:2, :])
    scale = jnp.sum(jnp.where(table, gate, 0.0), axis=1, keepdims=True)
    pick = table.astype(BF16)
    rows_in = jnp.dot(pick, tok_ref[...], preferred_element_type=F32)
    rows_dy = jnp.dot(pick, dy_ref[...], preferred_element_type=F32)
    out = jnp.where(row < CAP, rows_in, scale * rows_dy)
    out_ref[...] = out.astype(BF16).reshape(EXPERTS, MSG, COLS)


def forward_kernel(pos_ref, w_in_ref, w_out_ref, *refs):
    xs, (pgact_t_ref, pg_ref) = refs[:-2], refs[-2:]
    pre = jnp.zeros((ROWS, HID), F32)
    act_grad = jnp.zeros((ROWS, HID), F32)
    for own, sib, mine, other in pairs(pos_ref, xs):
        x = jnp.concatenate([own(), sib()], axis=1)
        w = jnp.concatenate([w_in_ref[pl.ds(mine, COLS), :], w_in_ref[pl.ds(other, COLS), :]], axis=0)
        v = jnp.concatenate([w_out_ref[:, pl.ds(mine, COLS)], w_out_ref[:, pl.ds(other, COLS)]], axis=1)
        pre = pre + jnp.dot(x, w, preferred_element_type=F32)
        act_grad = act_grad + lax.dot_general(x, v, CONTRACT_LAST, preferred_element_type=F32)
    act_grad = jnp.concatenate([act_grad[CAP:], act_grad[:CAP]], axis=0)
    act, pullback = jax.vjp(lambda v: jax.nn.gelu(v, approximate=True), pre)
    pre_grad = pullback(act_grad)[0]
    act = jnp.concatenate([act[ROWS - CAP:], act[:ROWS - CAP]], axis=0)
    row = lax.broadcasted_iota(jnp.int32, (EXPERTS, MSG, HID), 1).reshape(ROWS, HID)
    pre_grad = jnp.where(row < CAP, pre_grad, 0.0).astype(BF16)
    act = jnp.where(row < CAP, 0.0, act).astype(BF16)
    pgact_t_ref[...] = jnp.concatenate([pre_grad, act], axis=1).T
    block = lax.broadcasted_iota(jnp.int32, (EXPERTS, CAP, ROWS), 0).reshape(KEPT, ROWS)
    within = lax.broadcasted_iota(jnp.int32, (EXPERTS, CAP, ROWS), 1).reshape(KEPT, ROWS)
    keep = (lax.broadcasted_iota(jnp.int32, (KEPT, ROWS), 1) == block * MSG + within).astype(BF16)
    pg_ref[...] = jnp.dot(keep, pre_grad, preferred_element_type=F32).astype(BF16)


def pairs(pos_ref, xs):
    half = len(xs) // 2
    y, c = pos_ref[0], pos_ref[1]
    steps = (0, NY - 1, 1, 2)
    for i, step in enumerate(steps):
        at = lax.rem(y + step, NY)
        for zl in range(NZ):
            if i < 3:
                own, sib, k = xs[i], xs[half + i], zl
            else:
                own, sib, k = xs[3 + zl // 2], xs[half + 3 + zl // 2], zl % 2
            first = (at * NZ + zl) * NC
            mine = pl.multiple_of((first + c) * COLS, COLS)
            other = pl.multiple_of((first + 1 - c) * COLS, COLS)

            def reader(ref, k=k):
                return lambda: ref[k * EXPERTS:(k + 1) * EXPERTS].reshape(ROWS, COLS)

            yield reader(own), reader(sib), mine, other


def partial_kernel(pos_ref, w_in_ref, pg_ref, far_ref, near_ref):
    y, c = pos_ref[0], pos_ref[1]
    pg = pg_ref[...]
    for place, step in enumerate((2, 0, 1, 3)):
        at = lax.rem(y + step, NY)
        for zl in range(NZ):
            first = (at * NZ + zl) * NC
            mine = pl.multiple_of((first + c) * COLS, COLS)
            other = pl.multiple_of((first + 1 - c) * COLS, COLS)
            w = jnp.concatenate([w_in_ref[pl.ds(mine, COLS), :], w_in_ref[pl.ds(other, COLS), :]], axis=0)
            out = lax.dot_general(pg, w, CONTRACT_LAST, preferred_element_type=F32).astype(BF16)
            for core in range(NC):
                block = out[:, core * COLS:(core + 1) * COLS]
                if place == 0:
                    far_ref[core, zl] = block
                else:
                    near_ref[core, place - 1, zl] = block


def grads_kernel(pos_ref, pgact_t_ref, *refs):
    xs, (w_in_grad_ref, w_out_grad_ref) = refs[:-2], refs[-2:]
    left = pgact_t_ref[...]
    for own, sib, mine, other in pairs(pos_ref, xs):
        x = jnp.concatenate([own(), sib()], axis=1)
        both = jnp.dot(left, x, preferred_element_type=F32)
        grad_in = both[:HID].T.astype(BF16)
        grad_out = both[HID:].astype(BF16)
        w_in_grad_ref[pl.ds(mine, COLS), :] = grad_in[:COLS]
        w_in_grad_ref[pl.ds(other, COLS), :] = grad_in[COLS:]
        w_out_grad_ref[:, pl.ds(mine, COLS)] = grad_out[:, :COLS]
        w_out_grad_ref[:, pl.ds(other, COLS)] = grad_out[:, COLS:]


def combine_kernel(ids_ref, back_ref, out_ref):
    table, _, _ = slot_table(ids_ref[...], CAP, lambda q: q)
    total = back_ref[0:EXPERTS].astype(F32)
    for z in range(1, NZ):
        total = total + back_ref[z * EXPERTS:(z + 1) * EXPERTS].astype(F32)
    rows = total.reshape(KEPT, COLS).astype(BF16)
    out_ref[...] = lax.dot_general(
        table.astype(BF16), rows, CONTRACT_FIRST, preferred_element_type=F32
    ).astype(BF16)


def shape(*dims, kind=BF16):
    return jax.ShapeDtypeStruct(dims, kind)


SMEM = pl.BlockSpec(memory_space=pltpu.SMEM)
WHOLE = pl.BlockSpec(memory_space=pltpu.VMEM)


def run(kernel, outs, scalars, *args):
    specs = [SMEM] * scalars + [WHOLE] * (len(args) - scalars)
    out_specs = jax.tree.map(lambda _: WHOLE, outs)
    return pl.pallas_call(kernel, out_shape=outs, in_specs=specs, out_specs=out_specs, compiler_params=VMEM)(*args)


def ring(value, step):
    return lax.ppermute(value, "y", [(i, (i + step) % NY) for i in range(NY)])


def across(value):
    return lax.ppermute(value, "c", [(0, 1), (1, 0)])


def add(*parts):
    total = parts[0].astype(F32)
    for part in parts[1:]:
        total = total + part.astype(F32)
    return total.astype(BF16)


def on_device(tokens, out_grad, expert_ids, gate_weights, w_in, w_out):
    pos = jnp.stack([lax.axis_index("y"), lax.axis_index("c")]).astype(jnp.int32)
    ids, gate = expert_ids.T, gate_weights.T
    send = run(dispatch_kernel, shape(EXPERTS, MSG, COLS), 0, ids, gate, tokens, out_grad)
    received = lax.all_to_all(send, ("zh", "x"), 0, 0, tiled=True)
    own = lax.all_gather(received, "zl", axis=0, tiled=True)
    prev, after = ring(own, 1), ring(own, -1)
    cut = NZ // 2 * EXPERTS
    far_a, far_b = ring(prev[:cut], 1), ring(after[cut:], -1)
    mine = [own, prev, after, far_a, far_b]
    xs = mine + [across(x) for x in mine]
    w_in, w_out = w_in[0], w_out[0]
    pgact_t, pg = run(
        forward_kernel, (shape(2 * HID, ROWS), shape(KEPT, HID)), 1, pos, w_in, w_out, *xs
    )
    far, near = run(
        partial_kernel,
        (shape(NC, NZ, KEPT, COLS), shape(NC, NY - 1, NZ, KEPT, COLS)),
        1, pos, w_in, pg,
    )
    far = add(far[0], across(far[1]))
    near = add(near[0], across(near[1]))
    half = NZ // 2
    from_prev, from_after = ring(far[:half], 1), ring(far[half:], -1)
    up = jnp.concatenate([add(near[1, :half], from_prev), near[1, half:]])
    down = jnp.concatenate([near[2, :half], add(near[2, half:], from_after)])
    summed = add(near[0], ring(up, 1), ring(down, -1))
    back = lax.all_to_all(summed.reshape(NZ * EXPERTS, CAP, COLS), ("zl", "zh", "x"), 0, 0, tiled=True)
    tokens_grad = run(combine_kernel, shape(TOK, COLS), 0, ids, back)
    w_in_grad, w_out_grad = run(
        grads_kernel, (shape(*w_in.shape), shape(*w_out.shape)), 1, pos, pgact_t, *xs
    )
    return tokens_grad, w_in_grad[None], w_out_grad[None]


def solution(mesh):
    fine = Mesh(mesh.devices.reshape(NY, NZ, NC, NH, NX), ("y", "zl", "c", "zh", "x"))
    dp, expert = ("y", "zl", "c"), ("zh", "x")
    placed = (
        P(expert, dp),
        P(expert, dp),
        P(expert, None),
        P(expert, None),
        P(expert, None, dp),
        P(expert, dp, None),
    )
    return jax.shard_map(
        on_device,
        mesh=fine,
        in_specs=placed,
        out_specs=(P(expert, dp), P(expert, None, dp), P(expert, dp, None)),
        check_vma=False,
    )
```

```python
import jax
import jax.numpy as jnp
from jax import lax
from jax.experimental import pallas as pl
from jax.experimental.pallas import tpu as pltpu
from jax.sharding import Mesh, PartitionSpec as P

NY, NZ, NC, NH, NX = 4, 4, 2, 4, 4
EXPERTS = NH * NX
TOK = 128
CAP = 20
MSG = 2 * CAP
COLS = 128
HID = 128
ROWS = EXPERTS * MSG
KEPT = EXPERTS * CAP
BF16 = jnp.bfloat16
F32 = jnp.float32
VMEM = pltpu.CompilerParams(vmem_limit_bytes=56 * 1024 * 1024)
CONTRACT_LAST = (((1,), (1,)), ((), ()))
CONTRACT_FIRST = (((0,), (0,)), ((), ()))


def slot_table(ids, rows_each, slot_of):
    experts = lax.broadcasted_iota(jnp.int32, (EXPERTS, TOK), 0)
    named = (experts == ids[0:1, :]) | (experts == ids[1:2, :])
    earlier = lax.broadcasted_iota(jnp.int32, (TOK, TOK), 0) < lax.broadcasted_iota(jnp.int32, (TOK, TOK), 1)
    prior = jnp.dot(named.astype(BF16), earlier.astype(BF16), preferred_element_type=F32)
    place = jnp.where(named, prior, -1.0).astype(BF16)
    shape = (EXPERTS, rows_each, TOK)
    expert = lax.broadcasted_iota(jnp.int32, shape, 0).reshape(EXPERTS * rows_each, TOK)
    row = lax.broadcasted_iota(jnp.int32, shape, 1).reshape(EXPERTS * rows_each, TOK)
    spread = (expert[:, :EXPERTS] == lax.broadcasted_iota(jnp.int32, (EXPERTS * rows_each, EXPERTS), 1)).astype(BF16)
    place_of_row = jnp.dot(spread, place, preferred_element_type=F32)
    return place_of_row == slot_of(row).astype(F32), expert, row


def dispatch_kernel(ids_ref, gate_ref, tok_ref, dy_ref, out_ref):
    ids = ids_ref[...]
    table, expert, row = slot_table(ids, MSG, lambda q: jnp.where(q >= CAP, q - CAP, q))
    gate = jnp.where(expert == ids[0:1, :], gate_ref[0:1, :], gate_ref[1:2, :])
    scale = jnp.sum(jnp.where(table, gate, 0.0), axis=1, keepdims=True)
    pick = table.astype(BF16)
    rows_in = jnp.dot(pick, tok_ref[...], preferred_element_type=F32)
    rows_dy = jnp.dot(pick, dy_ref[...], preferred_element_type=F32)
    out = jnp.where(row < CAP, rows_in, scale * rows_dy)
    out_ref[...] = out.astype(BF16).reshape(EXPERTS, MSG, COLS)


def split_kernel(pos_ref, w_in_ref, w_out_ref, after_ref, in_other, out_other):
    del after_ref
    c = pos_ref[1]
    for k in range(NY * NZ):
        first = pl.multiple_of((k * NC + 1 - c) * COLS, COLS)
        in_other[k] = w_in_ref[pl.ds(first, COLS), :]
        out_other[:, k * COLS:(k + 1) * COLS] = w_out_ref[:, pl.ds(first, COLS)]


def places(y, c, step):
    return lax.rem(y + jnp.where(c == 0, NY - step, step), NY)


def chunk(ref, zl):
    return ref[zl * EXPERTS:(zl + 1) * EXPERTS].reshape(ROWS, COLS)


def joined(first, second):
    return jnp.concatenate([first, second], axis=1)


def weights_in(w_in_ref, sib_ref, c, k):
    mine = w_in_ref[pl.ds(pl.multiple_of((k * NC + c) * COLS, COLS), COLS), :]
    return joined(mine, sib_ref[k])


def weights_out(w_out_ref, sib_ref, c, k):
    mine = w_out_ref[:, pl.ds(pl.multiple_of((k * NC + c) * COLS, COLS), COLS)]
    return jnp.concatenate([mine, sib_ref[:, pl.ds(pl.multiple_of(k * COLS, COLS), COLS)]], axis=0)


def forward(pos_ref, w_in_ref, w_in_sib_ref, w_out_ref, w_out_sib_ref, xs):
    y, c = pos_ref[0], pos_ref[1]
    pre = jnp.zeros((ROWS, NC * HID), F32)
    act_grad = jnp.zeros((ROWS, NC * HID), F32)
    for step, blocks in xs:
        at = places(y, c, step) * NZ
        for zl in range(0, NZ, 2):
            x = joined(*[chunk(*block) for block in blocks[zl:zl + 2]])
            w = jnp.concatenate([weights_in(w_in_ref, w_in_sib_ref, c, at + z) for z in (zl, zl + 1)], axis=0)
            v = joined(*[weights_out(w_out_ref, w_out_sib_ref, c, at + z) for z in (zl, zl + 1)])
            pre = pre + jnp.dot(x, w, preferred_element_type=F32)
            act_grad = act_grad + lax.dot_general(x, v, CONTRACT_LAST, preferred_element_type=F32)
    row = lax.broadcasted_iota(jnp.int32, (EXPERTS, MSG, NC * HID), 1).reshape(ROWS, NC * HID)
    return jnp.where(row < CAP, pre, act_grad)


def whole(ref):
    return [(ref, z) for z in range(NZ)]


def halves(low, high):
    return [(low, 0), (low, 1), (high, 0), (high, 1)]


def forward_first_kernel(pos_ref, wi, wis, wo, wos, x0, a1, b1, out_ref):
    out_ref[...] = forward(pos_ref, wi, wis, wo, wos, [(0, whole(x0)), (1, halves(a1, b1))])


def forward_last_kernel(pos_ref, wi, wis, wo, wos, a2, b2, a3, b3, before_ref, out_ref):
    xs = [(2, halves(a2, b2)), (3, halves(a3, b3))]
    out_ref[...] = before_ref[...] + forward(pos_ref, wi, wis, wo, wos, xs)


def middle_kernel(pos_ref, w_in_ref, w_in_sib_ref, part_ref, part_sib_ref, pgact_t_ref, out_ref):
    c = pos_ref[1]
    sib = part_sib_ref[...]
    both = part_ref[...] + joined(sib[:, HID:], sib[:, :HID])
    act_grad = jnp.concatenate([both[CAP:], both[:CAP]], axis=0)
    act, pullback = jax.vjp(lambda v: jax.nn.gelu(v, approximate=True), both)
    pre_grad = pullback(act_grad)[0]
    act = jnp.concatenate([act[ROWS - CAP:], act[:ROWS - CAP]], axis=0)
    row = lax.broadcasted_iota(jnp.int32, (EXPERTS, MSG, NC * HID), 1).reshape(ROWS, NC * HID)
    pre_grad = jnp.where(row < CAP, pre_grad, 0.0).astype(BF16)
    act = jnp.where(row < CAP, 0.0, act).astype(BF16)
    pgact_t_ref[...] = joined(pre_grad, act).T
    block = lax.broadcasted_iota(jnp.int32, (EXPERTS, CAP, ROWS), 0).reshape(KEPT, ROWS)
    within = lax.broadcasted_iota(jnp.int32, (EXPERTS, CAP, ROWS), 1).reshape(KEPT, ROWS)
    keep = (lax.broadcasted_iota(jnp.int32, (KEPT, ROWS), 1) == block * MSG + within).astype(BF16)
    pg = jnp.dot(keep, pre_grad, preferred_element_type=F32).astype(BF16)
    for k in range(0, NY * NZ, 2):
        w = jnp.concatenate([weights_in(w_in_ref, w_in_sib_ref, c, j) for j in (k, k + 1)], axis=0)
        out = lax.dot_general(pg, w, CONTRACT_LAST, preferred_element_type=F32).astype(BF16)
        for j in range(2):
            out_ref[(k + j) // NZ, (k + j) % NZ] = out[:, j * COLS:(j + 1) * COLS]


def grads_kernel(pos_ref, pgact_t_ref, x0, a1, b1, a2, b2, a3, b3, in_mine, in_other, out_mine, out_other):
    y, c = pos_ref[0], pos_ref[1]
    left = pgact_t_ref[...]
    for step, blocks in enumerate((whole(x0), halves(a1, b1), halves(a2, b2), halves(a3, b3))):
        at = places(y, c, step) * NZ
        for zl in range(0, NZ, 2):
            x = joined(*[chunk(*block) for block in blocks[zl:zl + 2]])
            both = jnp.dot(left, x, preferred_element_type=F32).astype(BF16)
            lanes = pl.ds(pl.multiple_of((at + zl) * COLS, 2 * COLS), 2 * COLS)
            for ref, first in ((in_mine, 0), (in_other, HID)):
                turned = both[first:first + HID].T
                ref[at + zl] = turned[:COLS]
                ref[at + zl + 1] = turned[COLS:]
            for ref, first in ((out_mine, 2 * HID), (out_other, 3 * HID)):
                ref[:, lanes] = both[first:first + HID]


def merge_kernel(pos_ref, in_mine, in_sib, out_mine, out_sib, w_in_grad_ref, w_out_grad_ref):
    c = pos_ref[1]
    for k in range(NY * NZ):
        for ins, outs, core in ((in_mine, out_mine, c), (in_sib, out_sib, 1 - c)):
            first = pl.multiple_of((k * NC + core) * COLS, COLS)
            w_in_grad_ref[pl.ds(first, COLS), :] = ins[k]
            w_out_grad_ref[:, pl.ds(first, COLS)] = outs[:, k * COLS:(k + 1) * COLS]


def combine_kernel(ids_ref, back_ref, out_ref):
    table, _, _ = slot_table(ids_ref[...], CAP, lambda q: q)
    total = back_ref[0:EXPERTS].astype(F32)
    for z in range(1, NZ):
        total = total + back_ref[z * EXPERTS:(z + 1) * EXPERTS].astype(F32)
    rows = total.reshape(KEPT, COLS).astype(BF16)
    out_ref[...] = lax.dot_general(
        table.astype(BF16), rows, CONTRACT_FIRST, preferred_element_type=F32
    ).astype(BF16)


SMEM = pl.BlockSpec(memory_space=pltpu.SMEM)
WHOLE = pl.BlockSpec(memory_space=pltpu.VMEM)
UNREAD = pl.BlockSpec(memory_space=pl.ANY)


def shape(*dims, kind=BF16):
    return jax.ShapeDtypeStruct(dims, kind)


def held(*dims, kind=BF16):
    return pltpu.VMEM(dims, kind)


def keep(value):
    return pltpu.with_memory_space_constraint(value, pltpu.VMEM)


def run(kernel, outs, scalars, *args, unread=0):
    specs = [SMEM] * scalars + [WHOLE] * (len(args) - scalars - unread) + [UNREAD] * unread
    out_specs = jax.tree.map(lambda _: WHOLE, outs)
    return pl.pallas_call(kernel, out_shape=outs, in_specs=specs, out_specs=out_specs, compiler_params=VMEM)(*args)


def ring(value):
    steps = [(i * NC + c, (i + (1 if c == 0 else NY - 1)) % NY * NC + c) for i in range(NY) for c in range(NC)]
    return lax.ppermute(value, ("y", "c"), steps)


def across(value):
    return lax.ppermute(value, "c", [(0, 1), (1, 0)])


def on_device(tokens, out_grad, expert_ids, gate_weights, w_in, w_out):
    pos = jnp.stack([lax.axis_index("y"), lax.axis_index("c")]).astype(jnp.int32)
    ids, gate = expert_ids.T, gate_weights.T
    w_in, w_out = w_in[0], w_out[0]
    blocks = NY * NZ
    half_in, half_out = held(blocks, COLS, HID), held(HID, blocks * COLS)
    send = run(dispatch_kernel, shape(EXPERTS, MSG, COLS), 0, ids, gate, tokens, out_grad)
    w_in_other, w_out_other = run(split_kernel, (half_in, half_out), 1, pos, w_in, w_out, send, unread=1)
    w_in_sib, w_out_sib = across(w_in_other), across(w_out_other)
    received = lax.all_to_all(send, ("zh", "x"), 0, 0, tiled=True)
    received, w_in_sib, w_out_sib = lax.optimization_barrier((received, w_in_sib, w_out_sib))
    x0 = lax.all_gather(received, "zl", axis=0, tiled=True)
    w_in_sib, w_out_sib = keep(w_in_sib), keep(w_out_sib)
    weights = (pos, w_in, w_in_sib, w_out, w_out_sib)
    cut = NZ // 2 * EXPERTS
    xs, a, b = [keep(x0)], x0[:cut], x0[cut:]
    for _ in range(NY - 1):
        a, b = ring(a), ring(b)
        xs += [keep(a), keep(b)]
    part = held(ROWS, NC * HID, kind=F32)
    first = run(forward_first_kernel, part, 1, *weights, *xs[:3])
    part = run(forward_last_kernel, part, 1, *weights, *xs[3:], keep(first))
    pgact_t, partial_rows = run(
        middle_kernel,
        (held(2 * NC * HID, ROWS), held(NY, NZ, KEPT, COLS)),
        1, pos, w_in, w_in_sib, keep(part), keep(across(part)),
    )
    parts = lax.all_to_all(partial_rows, "y", 0, 0, tiled=True)
    summed = jnp.sum(parts.astype(F32), axis=0).astype(BF16)
    back = lax.all_to_all(summed.reshape(NZ * EXPERTS, CAP, COLS), ("zl", "zh", "x"), 0, 0, tiled=True)
    tokens_grad = run(combine_kernel, shape(TOK, COLS), 0, ids, keep(back))
    in_mine, in_other, out_mine, out_other = run(
        grads_kernel, (half_in, half_in, half_out, half_out), 1, pos, keep(pgact_t), *xs
    )
    w_in_grad, w_out_grad = run(
        merge_kernel, (shape(*w_in.shape), shape(*w_out.shape)),
        1, pos, keep(in_mine), keep(across(in_other)), keep(out_mine), keep(across(out_other)),
    )
    return tokens_grad, w_in_grad[None], w_out_grad[None]


def solution(mesh):
    fine = Mesh(mesh.devices.reshape(NY, NZ, NC, NH, NX), ("y", "zl", "c", "zh", "x"))
    dp, expert = ("y", "zl", "c"), ("zh", "x")
    placed = (
        P(expert, dp),
        P(expert, dp),
        P(expert, None),
        P(expert, None),
        P(expert, None, dp),
        P(expert, dp, None),
    )
    return jax.shard_map(
        on_device,
        mesh=fine,
        in_specs=placed,
        out_specs=(P(expert, dp), P(expert, None, dp), P(expert, dp, None)),
        check_vma=False,
    )
```

```python
import jax
import jax.numpy as jnp
from jax import lax
from jax.experimental import pallas as pl
from jax.experimental.pallas import tpu as pltpu
from jax.sharding import Mesh, PartitionSpec as P

NY, NZ, NC, NH, NX = 4, 4, 2, 4, 4
EXPERTS = NH * NX
TOK = 128
CAP = 20
MSG = 2 * CAP
COLS = 128
HID = 128
ROWS = EXPERTS * MSG
KEPT = EXPERTS * CAP
BF16 = jnp.bfloat16
F32 = jnp.float32
VMEM = pltpu.CompilerParams(vmem_limit_bytes=24 * 1024 * 1024)
CONTRACT_LAST = (((1,), (1,)), ((), ()))
CONTRACT_FIRST = (((0,), (0,)), ((), ()))


def slot_table(ids, rows_each, slot_of):
    experts = lax.broadcasted_iota(jnp.int32, (EXPERTS, TOK), 0)
    named = (experts == ids[0:1, :]) | (experts == ids[1:2, :])
    earlier = lax.broadcasted_iota(jnp.int32, (TOK, TOK), 0) < lax.broadcasted_iota(jnp.int32, (TOK, TOK), 1)
    prior = jnp.dot(named.astype(BF16), earlier.astype(BF16), preferred_element_type=F32)
    place = jnp.where(named, prior, -1.0).astype(BF16)
    shape = (EXPERTS, rows_each, TOK)
    expert = lax.broadcasted_iota(jnp.int32, shape, 0).reshape(EXPERTS * rows_each, TOK)
    row = lax.broadcasted_iota(jnp.int32, shape, 1).reshape(EXPERTS * rows_each, TOK)
    spread = (expert[:, :EXPERTS] == lax.broadcasted_iota(jnp.int32, (EXPERTS * rows_each, EXPERTS), 1)).astype(BF16)
    place_of_row = jnp.dot(spread, place, preferred_element_type=F32)
    return place_of_row == slot_of(row).astype(F32), expert, row


def dispatch_kernel(ids_ref, gate_ref, tok_ref, dy_ref, out_ref):
    ids = ids_ref[...]
    table, expert, row = slot_table(ids, MSG, lambda q: jnp.where(q >= CAP, q - CAP, q))
    gate = jnp.where(expert == ids[0:1, :], gate_ref[0:1, :], gate_ref[1:2, :])
    scale = jnp.sum(jnp.where(table, gate, 0.0), axis=1, keepdims=True)
    pick = table.astype(BF16)
    rows_in = jnp.dot(pick, tok_ref[...], preferred_element_type=F32)
    rows_dy = jnp.dot(pick, dy_ref[...], preferred_element_type=F32)
    out = jnp.where(row < CAP, rows_in, scale * rows_dy)
    out_ref[...] = out.astype(BF16).reshape(EXPERTS, MSG, COLS)


def split_kernel(pos_ref, w_in_ref, w_out_ref, after_ref, in_ref, out_ref, sems):
    del after_ref
    other = 1 - pos_ref[1]
    blocks = NY * NZ
    copies = [pltpu.make_async_copy(w_in_ref.at[:, other], in_ref, sems.at[blocks])]
    for k in range(blocks):
        columns = pl.ds(pl.multiple_of((k * NC + other) * COLS, COLS), COLS)
        copies.append(pltpu.make_async_copy(w_out_ref.at[:, columns], out_ref.at[k], sems.at[k]))
    for copy in copies:
        copy.start()
    for copy in copies:
        copy.wait()


def table_kernel(ids_ref, after_ref, table_ref):
    del after_ref
    table, _, _ = slot_table(ids_ref[...], CAP, lambda q: q)
    table_ref[...] = table.astype(BF16)


def places(y, c):
    near, far = y + 1 - 2 * lax.rem(y, 2), NY - 1 - y
    return y, jnp.where(c == 0, near, far), jnp.where(c == 0, far, near), lax.rem(y + 2, NY)


def chunk(ref, zl):
    return ref[zl * EXPERTS:(zl + 1) * EXPERTS].reshape(ROWS, COLS)


def joined(first, second):
    return jnp.concatenate([first, second], axis=1)


def weights_in(w_in_ref, sib_ref, c, k):
    mine = w_in_ref[pl.ds(pl.multiple_of((k * NC + c) * COLS, COLS), COLS), :]
    return joined(mine, sib_ref[k])


def weights_out(w_out_ref, sib_ref, c, k):
    mine = w_out_ref[:, pl.ds(pl.multiple_of((k * NC + c) * COLS, COLS), COLS)]
    return jnp.concatenate([mine, sib_ref[k]], axis=0)


def forward(pos_ref, w_in_ref, w_out_ref, in_sib_ref, out_sib_ref, xs):
    c = pos_ref[1]
    at_of = places(pos_ref[0], c)
    pre = jnp.zeros((ROWS, NC * HID), F32)
    act_grad = jnp.zeros((ROWS, NC * HID), F32)
    for place, blocks in xs:
        at = at_of[place] * NZ
        for zl in range(0, NZ, 2):
            x = joined(chunk(*blocks[zl]), chunk(*blocks[zl + 1]))
            w = jnp.concatenate([weights_in(w_in_ref, in_sib_ref, c, at + z) for z in (zl, zl + 1)], axis=0)
            v = joined(*[weights_out(w_out_ref, out_sib_ref, c, at + z) for z in (zl, zl + 1)])
            pre = pre + jnp.dot(x, w, preferred_element_type=F32)
            act_grad = act_grad + lax.dot_general(x, v, CONTRACT_LAST, preferred_element_type=F32)
    row = lax.broadcasted_iota(jnp.int32, (EXPERTS, MSG, NC * HID), 1).reshape(ROWS, NC * HID)
    return jnp.where(row < CAP, pre, act_grad)


def whole(ref):
    return [(ref, z) for z in range(NZ)]


def halves(low, high):
    return [(low, 0), (low, 1), (high, 0), (high, 1)]


def forward_first_kernel(pos_ref, wi, wo, wis, wos, own, first_a, first_b, out_ref):
    out_ref[...] = forward(pos_ref, wi, wo, wis, wos, [(0, whole(own)), (1, halves(first_a, first_b))])


def forward_second_kernel(pos_ref, wi, wo, wis, wos, second_a, second_b, before_ref, out_ref):
    out_ref[...] = before_ref[...] + forward(pos_ref, wi, wo, wis, wos, [(2, halves(second_a, second_b))])


def forward_last_kernel(pos_ref, wi, wo, wis, wos, last_a, last_b, before_ref, out_ref, sent_ref):
    total = before_ref[...] + forward(pos_ref, wi, wo, wis, wos, [(3, halves(last_a, last_b))])
    out_ref[...] = total
    sent_ref[...] = total.astype(BF16)


def middle_kernel(pos_ref, w_in_ref, sib_ref, part_ref, part_sib_ref, pgact_ref, *outs):
    c = pos_ref[1]
    passed = part_sib_ref[...]
    both = part_ref[...] + joined(passed[:, HID:], passed[:, :HID]).astype(F32)
    act_grad = jnp.concatenate([both[CAP:], both[:CAP]], axis=0)
    act, pullback = jax.vjp(lambda v: jax.nn.gelu(v, approximate=True), both)
    pre_grad = pullback(act_grad)[0]
    act = jnp.concatenate([act[ROWS - CAP:], act[:ROWS - CAP]], axis=0)
    row = lax.broadcasted_iota(jnp.int32, (EXPERTS, MSG, NC * HID), 1).reshape(ROWS, NC * HID)
    pre_grad = jnp.where(row < CAP, pre_grad, 0.0).astype(BF16)
    act = jnp.where(row < CAP, 0.0, act).astype(BF16)
    pgact_ref[...] = joined(pre_grad, act)
    block = lax.broadcasted_iota(jnp.int32, (EXPERTS, CAP, ROWS), 0).reshape(KEPT, ROWS)
    within = lax.broadcasted_iota(jnp.int32, (EXPERTS, CAP, ROWS), 1).reshape(KEPT, ROWS)
    keep = (lax.broadcasted_iota(jnp.int32, (KEPT, ROWS), 1) == block * MSG + within).astype(BF16)
    pg = jnp.dot(keep, pre_grad, preferred_element_type=F32).astype(BF16)
    for at, out_ref in zip(places(pos_ref[0], c), outs):
        for zl in range(0, NZ, 2):
            w = jnp.concatenate([weights_in(w_in_ref, sib_ref, c, at * NZ + z) for z in (zl, zl + 1)], axis=0)
            out = lax.dot_general(pg, w, CONTRACT_LAST, preferred_element_type=F32).astype(BF16)
            for j in range(2):
                out_ref[zl + j] = out[:, j * COLS:(j + 1) * COLS]


def relay_kernel(mine_ref, passed_ref, out_ref):
    out_ref[...] = (mine_ref[...].astype(F32) + passed_ref[...].astype(F32)).astype(BF16)


def total_kernel(mine_ref, first_ref, second_ref, out_ref):
    for zl in range(NZ):
        total = mine_ref[zl].astype(F32) + first_ref[zl].astype(F32) + second_ref[zl].astype(F32)
        out_ref[zl * EXPERTS:(zl + 1) * EXPERTS] = total.reshape(EXPERTS, CAP, COLS).astype(BF16)


def grads_kernel(pos_ref, pgact_ref, *refs):
    xs, (in_mine, out_mine, in_other, out_other) = refs[:7], refs[8:]
    left = pgact_ref[...].T
    xs = [whole(xs[0])] + [halves(*xs[i:i + 2]) for i in (1, 3, 5)]
    for y, blocks in zip(places(pos_ref[0], pos_ref[1]), xs):
        at = y * NZ
        for zl in range(0, NZ, 2):
            x = joined(chunk(*blocks[zl]), chunk(*blocks[zl + 1]))
            both = jnp.dot(left, x, preferred_element_type=F32).astype(BF16)
            for ref, first in ((in_mine, 0), (in_other, HID)):
                turned = both[first:first + HID].T
                ref[at + zl] = turned[:COLS]
                ref[at + zl + 1] = turned[COLS:]
            lanes = pl.ds(pl.multiple_of((at + zl) * COLS, 2 * COLS), 2 * COLS)
            out_mine[:, lanes] = both[2 * HID:3 * HID]
            for j in range(2):
                out_other[at + zl + j] = both[3 * HID:, j * COLS:(j + 1) * COLS]


def merge_kernel(pos_ref, in_mine, out_mine, in_sib, out_sib, w_in_grad_ref, w_out_grad_ref):
    c = pos_ref[1]
    blocks = NY * NZ
    for k in range(blocks):
        mine = pl.ds(pl.multiple_of((k * NC + c) * COLS, COLS), COLS)
        other = pl.ds(pl.multiple_of((k * NC + 1 - c) * COLS, COLS), COLS)
        w_in_grad_ref[mine, :] = in_mine[k]
        w_in_grad_ref[other, :] = in_sib[k]
        w_out_grad_ref[:, mine] = out_mine[:, k * COLS:(k + 1) * COLS]
        w_out_grad_ref[:, other] = out_sib[k]


def combine_kernel(table_ref, back_ref, out_ref):
    total = back_ref[0:EXPERTS].astype(F32)
    for z in range(1, NZ):
        total = total + back_ref[z * EXPERTS:(z + 1) * EXPERTS].astype(F32)
    rows = total.reshape(KEPT, COLS).astype(BF16)
    out_ref[...] = lax.dot_general(table_ref[...], rows, CONTRACT_FIRST, preferred_element_type=F32).astype(BF16)


SMEM = pl.BlockSpec(memory_space=pltpu.SMEM)
WHOLE = pl.BlockSpec(memory_space=pltpu.VMEM)
UNREAD = pl.BlockSpec(memory_space=pl.ANY)


def shape(*dims, kind=BF16):
    return jax.ShapeDtypeStruct(dims, kind)


def held(*dims, kind=BF16):
    return pltpu.VMEM(dims, kind)


def keep(value):
    return pltpu.with_memory_space_constraint(value, pltpu.VMEM)


def far(value):
    return pltpu.with_memory_space_constraint(value, pltpu.HBM)


def run(kernel, outs, scalars, *args, unread=0, scratch=()):
    specs = [SMEM] * scalars + [WHOLE] * (len(args) - scalars - unread) + [UNREAD] * unread
    out_specs = jax.tree.map(lambda _: WHOLE, outs)
    return pl.pallas_call(
        kernel, out_shape=outs, in_specs=specs, out_specs=out_specs, scratch_shapes=scratch, compiler_params=VMEM
    )(*args)


def partner(value, which):
    near, far = [i ^ 1 for i in range(NY)], [NY - 1 - i for i in range(NY)]
    to = [(near, far), (far, near)]
    return lax.ppermute(value, ("y", "c"), [(i * NC + c, to[c][which][i] * NC + c) for i in range(NY) for c in range(NC)])


def across(value):
    return lax.ppermute(value, "c", [(0, 1), (1, 0)])


def on_device(tokens, out_grad, expert_ids, gate_weights, w_in, w_out):
    pos = jnp.stack([lax.axis_index("y"), lax.axis_index("c")]).astype(jnp.int32)
    ids, gate = far(expert_ids.T), far(gate_weights.T)
    w_in, w_out = w_in[0], w_out[0]
    blocks = NY * NZ
    half_in, half_out = held(blocks, COLS, HID), held(HID, blocks * COLS)
    send = run(dispatch_kernel, shape(EXPERTS, MSG, COLS), 0, ids, gate, far(tokens), far(out_grad))
    in_other, out_other = run(
        split_kernel, (half_in, half_in), 1, pos, far(w_in.reshape(blocks, NC, COLS, HID)), far(w_out), send,
        unread=3, scratch=[pltpu.SemaphoreType.DMA((blocks + 1,))],
    )
    in_sib, out_sib = across(in_other), across(out_other)
    received = lax.all_to_all(send, ("zh", "x"), 0, 0, tiled=True)
    received, in_sib, out_sib = lax.optimization_barrier((received, in_sib, out_sib))
    own = lax.all_gather(received, "zl", axis=0, tiled=True)
    weights = (pos, w_in, w_out, keep(in_sib), keep(out_sib))
    cut = NZ // 2 * EXPERTS
    low, high = own[:cut], own[cut:]
    first_a, second_b = partner(low, 0), partner(high, 1)
    first_b, second_a = partner(high, 0), partner(low, 1)
    last_a, last_b = partner(first_a, 1), partner(second_b, 0)
    xs = [keep(x) for x in (own, first_a, first_b, second_a, second_b, last_a, last_b)]
    part = held(ROWS, NC * HID, kind=F32)
    some = run(forward_first_kernel, part, 1, *weights, *xs[:3])
    more = run(forward_second_kernel, part, 1, *weights, *xs[3:5], keep(some))
    mine, sent = run(
        forward_last_kernel, (part, held(ROWS, NC * HID)), 1, *weights, *xs[5:], keep(more)
    )
    rows = held(NZ, KEPT, COLS)
    pgact, to_own, to_first, to_second, to_last = run(
        middle_kernel,
        (pltpu.HBM((ROWS, 2 * NC * HID), BF16), rows, rows, rows, rows),
        1, pos, w_in, keep(in_sib), keep(mine), keep(across(sent)),
    )
    passed, from_second = partner(to_last, 1), partner(to_second, 1)
    from_first = partner(run(relay_kernel, rows, 0, keep(to_first), keep(passed)), 0)
    summed = run(total_kernel, held(NZ * EXPERTS, CAP, COLS), 0, keep(to_own), keep(from_first), keep(from_second))
    table = run(table_kernel, held(KEPT, TOK), 0, ids, summed, unread=1)
    back = lax.all_to_all(summed, ("zl", "zh", "x"), 0, 0, tiled=True)
    tokens_grad = run(combine_kernel, shape(TOK, COLS), 0, keep(table), keep(back))
    in_mine, out_mine, in_other, out_other = run(
        grads_kernel, (half_in, half_out, half_in, half_in), 1, pos, pgact, *xs, summed, unread=1
    )
    w_in_grad, w_out_grad = run(
        merge_kernel, (shape(*w_in.shape), shape(*w_out.shape)),
        1, pos, keep(in_mine), keep(out_mine), keep(across(in_other)), keep(across(out_other)),
    )
    return tokens_grad, w_in_grad[None], w_out_grad[None]


def solution(mesh):
    fine = Mesh(mesh.devices.reshape(NY, NZ, NC, NH, NX), ("y", "zl", "c", "zh", "x"))
    dp, expert = ("y", "zl", "c"), ("zh", "x")
    placed = (
        P(expert, dp),
        P(expert, dp),
        P(expert, None),
        P(expert, None),
        P(expert, None, dp),
        P(expert, dp, None),
    )
    return jax.shard_map(
        on_device,
        mesh=fine,
        in_specs=placed,
        out_specs=(P(expert, dp), P(expert, None, dp), P(expert, dp, None)),
        check_vma=False,
    )
```

```python
import jax
import jax.numpy as jnp
from jax import lax
from jax.experimental import pallas as pl
from jax.experimental.pallas import tpu as pltpu
from jax.sharding import Mesh, PartitionSpec as P

NY, NZ, NC, NH, NX = 4, 4, 2, 4, 4
EXPERTS = NH * NX
TOK = 128
CAP = 20
MSG = 2 * CAP
COLS = 128
HID = 128
ROWS = EXPERTS * MSG
KEPT = EXPERTS * CAP
BF16 = jnp.bfloat16
F32 = jnp.float32
VMEM = pltpu.CompilerParams(vmem_limit_bytes=14 * 1024 * 1024)
CONTRACT_LAST = (((1,), (1,)), ((), ()))
CONTRACT_FIRST = (((0,), (0,)), ((), ()))


def slot_table(ids, rows_each, slot_of):
    experts = lax.broadcasted_iota(jnp.int32, (EXPERTS, TOK), 0)
    named = (experts == ids[0:1, :]) | (experts == ids[1:2, :])
    earlier = lax.broadcasted_iota(jnp.int32, (TOK, TOK), 0) < lax.broadcasted_iota(jnp.int32, (TOK, TOK), 1)
    prior = jnp.dot(named.astype(BF16), earlier.astype(BF16), preferred_element_type=F32)
    place = jnp.where(named, prior, -1.0).astype(BF16)
    shape = (EXPERTS, rows_each, TOK)
    expert = lax.broadcasted_iota(jnp.int32, shape, 0).reshape(EXPERTS * rows_each, TOK)
    row = lax.broadcasted_iota(jnp.int32, shape, 1).reshape(EXPERTS * rows_each, TOK)
    spread = (expert[:, :EXPERTS] == lax.broadcasted_iota(jnp.int32, (EXPERTS * rows_each, EXPERTS), 1)).astype(BF16)
    place_of_row = jnp.dot(spread, place, preferred_element_type=F32)
    return place_of_row == slot_of(row).astype(F32), expert, row


def dispatch_kernel(ids_ref, gate_ref, tok_ref, dy_ref, out_ref):
    ids = ids_ref[...]
    table, expert, row = slot_table(ids, MSG, lambda q: jnp.where(q >= CAP, q - CAP, q))
    gate = jnp.where(expert == ids[0:1, :], gate_ref[0:1, :], gate_ref[1:2, :])
    scale = jnp.sum(jnp.where(table, gate, 0.0), axis=1, keepdims=True)
    pick = table.astype(BF16)
    rows_in = jnp.dot(pick, tok_ref[...], preferred_element_type=F32)
    rows_dy = jnp.dot(pick, dy_ref[...], preferred_element_type=F32)
    out = jnp.where(row < CAP, rows_in, scale * rows_dy)
    out_ref[...] = out.astype(BF16).reshape(EXPERTS, MSG, COLS)


def split_kernel(w_in_ref, w_out_ref, after_ref, in_ref, out_ref, sems):
    del after_ref
    other = 1 - position()[1]
    blocks = NY * NZ
    copies = [pltpu.make_async_copy(w_in_ref.at[:, other], in_ref, sems.at[blocks])]
    for k in range(blocks):
        columns = pl.ds(pl.multiple_of((k * NC + other) * COLS, COLS), COLS)
        copies.append(pltpu.make_async_copy(w_out_ref.at[:, columns], out_ref.at[k], sems.at[k]))
    for copy in copies:
        copy.start()
    for copy in copies:
        copy.wait()


def table_kernel(ids_ref, after_ref, table_ref):
    del after_ref
    table, _, _ = slot_table(ids_ref[...], CAP, lambda q: q)
    table_ref[...] = table.astype(BF16)


def position():
    return lax.axis_index("y"), lax.axis_index("c")


def places(y, c):
    near, far = y + 1 - 2 * lax.rem(y, 2), NY - 1 - y
    return y, jnp.where(c == 0, near, far), jnp.where(c == 0, far, near), lax.rem(y + 2, NY)


def chunk(ref, zl):
    return ref[zl * EXPERTS:(zl + 1) * EXPERTS].reshape(ROWS, COLS)


def joined(first, second):
    return jnp.concatenate([first, second], axis=1)


def weights_in(w_in_ref, sib_ref, c, k):
    mine = w_in_ref[pl.ds(pl.multiple_of((k * NC + c) * COLS, COLS), COLS), :]
    return joined(mine, sib_ref[k])


def weights_out(w_out_ref, sib_ref, c, k):
    mine = w_out_ref[:, pl.ds(pl.multiple_of((k * NC + c) * COLS, COLS), COLS)]
    return jnp.concatenate([mine, sib_ref[k]], axis=0)


def forward(w_in_ref, w_out_ref, in_sib_ref, out_sib_ref, xs):
    _, c = position()
    at_of = places(position()[0], c)
    pre = jnp.zeros((ROWS, NC * HID), F32)
    act_grad = jnp.zeros((ROWS, NC * HID), F32)
    for place, blocks in xs:
        at = at_of[place] * NZ
        for zl in range(0, NZ, 2):
            x = joined(chunk(*blocks[zl]), chunk(*blocks[zl + 1]))
            w = jnp.concatenate([weights_in(w_in_ref, in_sib_ref, c, at + z) for z in (zl, zl + 1)], axis=0)
            v = joined(*[weights_out(w_out_ref, out_sib_ref, c, at + z) for z in (zl, zl + 1)])
            pre = pre + jnp.dot(x, w, preferred_element_type=F32)
            act_grad = act_grad + lax.dot_general(x, v, CONTRACT_LAST, preferred_element_type=F32)
    row = lax.broadcasted_iota(jnp.int32, (EXPERTS, MSG, NC * HID), 1).reshape(ROWS, NC * HID)
    return jnp.where(row < CAP, pre, act_grad)


def whole(ref):
    return [(ref, z) for z in range(NZ)]


def halves(low, high):
    return [(low, 0), (low, 1), (high, 0), (high, 1)]


def forward_first_kernel(wi, wo, wis, wos, own, first_a, first_b, out_ref):
    out_ref[...] = forward(wi, wo, wis, wos, [(0, whole(own)), (1, halves(first_a, first_b))])


def forward_second_kernel(wi, wo, wis, wos, second_a, second_b, before_ref, out_ref):
    out_ref[...] = before_ref[...] + forward(wi, wo, wis, wos, [(2, halves(second_a, second_b))])


def forward_last_kernel(wi, wo, wis, wos, last_a, last_b, before_ref, out_ref, sent_ref):
    total = before_ref[...] + forward(wi, wo, wis, wos, [(3, halves(last_a, last_b))])
    out_ref[...] = total
    sent_ref[...] = total.astype(BF16)


def activations(part_ref, part_sib_ref):
    passed = part_sib_ref[...]
    both = part_ref[...] + joined(passed[:, HID:], passed[:, :HID]).astype(F32)
    act_grad = jnp.concatenate([both[CAP:], both[:CAP]], axis=0)
    act, pullback = jax.vjp(lambda v: jax.nn.gelu(v, approximate=True), both)
    pre_grad = pullback(act_grad)[0]
    act = jnp.concatenate([act[ROWS - CAP:], act[:ROWS - CAP]], axis=0)
    row = lax.broadcasted_iota(jnp.int32, (EXPERTS, MSG, NC * HID), 1).reshape(ROWS, NC * HID)
    return jnp.where(row < CAP, pre_grad, 0.0).astype(BF16), jnp.where(row < CAP, 0.0, act).astype(BF16)


def middle_kernel(w_in_ref, sib_ref, part_ref, part_sib_ref, *outs):
    y, c = position()
    pre_grad, _ = activations(part_ref, part_sib_ref)
    block = lax.broadcasted_iota(jnp.int32, (EXPERTS, CAP, ROWS), 0).reshape(KEPT, ROWS)
    within = lax.broadcasted_iota(jnp.int32, (EXPERTS, CAP, ROWS), 1).reshape(KEPT, ROWS)
    keep = (lax.broadcasted_iota(jnp.int32, (KEPT, ROWS), 1) == block * MSG + within).astype(BF16)
    pg = jnp.dot(keep, pre_grad, preferred_element_type=F32).astype(BF16)
    for at, out_ref in zip(places(y, c), outs):
        for zl in range(0, NZ, 2):
            w = jnp.concatenate([weights_in(w_in_ref, sib_ref, c, at * NZ + z) for z in (zl, zl + 1)], axis=0)
            out = lax.dot_general(pg, w, CONTRACT_LAST, preferred_element_type=F32).astype(BF16)
            for j in range(2):
                out_ref[zl + j] = out[:, j * COLS:(j + 1) * COLS]


def relay_kernel(mine_ref, passed_ref, out_ref):
    out_ref[...] = (mine_ref[...].astype(F32) + passed_ref[...].astype(F32)).astype(BF16)


def total_kernel(mine_ref, first_ref, second_ref, after_ref, out_ref):
    del after_ref
    out_ref[...] = (mine_ref[...].astype(F32) + first_ref[...].astype(F32) + second_ref[...].astype(F32)).astype(BF16)


def gathered_kernel(parts_ref, out_ref):
    total = parts_ref[0].astype(F32)
    for zl in range(1, NZ):
        total = total + parts_ref[zl].astype(F32)
    out_ref[...] = total.reshape(EXPERTS, CAP, COLS).astype(BF16)


def grads_kernel(part_ref, part_sib_ref, *refs):
    xs, (in_mine, out_mine, in_other, out_other) = refs[:7], refs[8:]
    left = joined(*activations(part_ref, part_sib_ref)).T
    xs = [whole(xs[0])] + [halves(*xs[i:i + 2]) for i in (1, 3, 5)]
    for y, blocks in zip(places(*position()), xs):
        at = y * NZ
        for zl in range(0, NZ, 2):
            x = joined(chunk(*blocks[zl]), chunk(*blocks[zl + 1]))
            both = jnp.dot(left, x, preferred_element_type=F32).astype(BF16)
            for ref, first in ((in_mine, 0), (in_other, HID)):
                turned = both[first:first + HID].T
                ref[at + zl] = turned[:COLS]
                ref[at + zl + 1] = turned[COLS:]
            lanes = pl.ds(pl.multiple_of((at + zl) * COLS, 2 * COLS), 2 * COLS)
            out_mine[:, lanes] = both[2 * HID:3 * HID]
            for j in range(2):
                out_other[at + zl + j] = both[3 * HID:, j * COLS:(j + 1) * COLS]


def merge_kernel(in_mine, out_mine, in_sib, out_sib, w_in_grad_ref, w_out_grad_ref):
    _, c = position()
    blocks = NY * NZ
    for k in range(blocks):
        mine = pl.ds(pl.multiple_of((k * NC + c) * COLS, COLS), COLS)
        other = pl.ds(pl.multiple_of((k * NC + 1 - c) * COLS, COLS), COLS)
        w_in_grad_ref[mine, :] = in_mine[k]
        w_in_grad_ref[other, :] = in_sib[k]
        w_out_grad_ref[:, mine] = out_mine[:, k * COLS:(k + 1) * COLS]
        w_out_grad_ref[:, other] = out_sib[k]


def combine_kernel(table_ref, back_ref, out_ref):
    rows = back_ref[...].astype(F32).reshape(KEPT, COLS).astype(BF16)
    out_ref[...] = lax.dot_general(table_ref[...], rows, CONTRACT_FIRST, preferred_element_type=F32).astype(BF16)


SMEM = pl.BlockSpec(memory_space=pltpu.SMEM)
WHOLE = pl.BlockSpec(memory_space=pltpu.VMEM)
UNREAD = pl.BlockSpec(memory_space=pl.ANY)


def shape(*dims, kind=BF16):
    return jax.ShapeDtypeStruct(dims, kind)


def held(*dims, kind=BF16):
    return pltpu.VMEM(dims, kind)


def keep(value):
    return pltpu.with_memory_space_constraint(value, pltpu.VMEM)


def far(value):
    return pltpu.with_memory_space_constraint(value, pltpu.HBM)


def run(kernel, outs, scalars, *args, unread=0, scratch=()):
    specs = [SMEM] * scalars + [WHOLE] * (len(args) - scalars - unread) + [UNREAD] * unread
    out_specs = jax.tree.map(lambda _: WHOLE, outs)
    return pl.pallas_call(
        kernel, out_shape=outs, in_specs=specs, out_specs=out_specs, scratch_shapes=scratch, compiler_params=VMEM
    )(*args)


def partner(value, which):
    near, far = [i ^ 1 for i in range(NY)], [NY - 1 - i for i in range(NY)]
    to = [(near, far), (far, near)]
    return lax.ppermute(value, ("y", "c"), [(i * NC + c, to[c][which][i] * NC + c) for i in range(NY) for c in range(NC)])


def across(value):
    return lax.ppermute(value, "c", [(0, 1), (1, 0)])


def on_device(tokens, out_grad, expert_ids, gate_weights, w_in, w_out):
    ids, gate = far(expert_ids.T), far(gate_weights.T)
    w_in, w_out = w_in[0], w_out[0]
    blocks = NY * NZ
    half_in, half_out = held(blocks, COLS, HID), held(HID, blocks * COLS)
    send = run(dispatch_kernel, shape(EXPERTS, MSG, COLS), 0, ids, gate, far(tokens), far(out_grad))
    in_other, out_other = run(
        split_kernel, (half_in, half_in), 0, far(w_in.reshape(blocks, NC, COLS, HID)), far(w_out), send,
        unread=3, scratch=[pltpu.SemaphoreType.DMA((blocks + 1,))],
    )
    in_sib, out_sib = across(in_other), across(out_other)
    received = lax.all_to_all(send, ("zh", "x"), 0, 0, tiled=True)
    received, in_sib, out_sib = lax.optimization_barrier((received, in_sib, out_sib))
    own = lax.all_gather(received, "zl", axis=0, tiled=True)
    weights = (w_in, w_out, keep(in_sib), keep(out_sib))
    cut = NZ // 2 * EXPERTS
    low, high = own[:cut], own[cut:]
    first_a, second_b = partner(low, 0), partner(high, 1)
    first_b, second_a = partner(high, 0), partner(low, 1)
    last_a, last_b = partner(first_a, 1), partner(second_b, 0)
    xs = [keep(x) for x in (own, first_a, first_b, second_a, second_b, last_a, last_b)]
    part = held(ROWS, NC * HID, kind=F32)
    some = run(forward_first_kernel, part, 0, *weights, *xs[:3])
    more = run(forward_second_kernel, part, 0, *weights, *xs[3:5], keep(some))
    mine, sent = run(
        forward_last_kernel, (part, held(ROWS, NC * HID)), 0, *weights, *xs[5:], keep(more)
    )
    rows = held(NZ, KEPT, COLS)
    parts = keep(mine), keep(across(sent))
    to_own, to_first, to_second, to_last = run(
        middle_kernel, (rows, rows, rows, rows), 0, w_in, keep(in_sib), *parts
    )
    passed, from_second = partner(to_last, 1), partner(to_second, 1)
    relayed = run(relay_kernel, rows, 0, keep(to_first), keep(passed))
    from_first = partner(relayed, 0)
    in_mine, out_mine, in_other, out_other = run(
        grads_kernel, (half_in, half_out, half_in, half_in), 0, *parts, *xs, relayed, unread=1
    )
    summed = run(total_kernel, rows, 0, keep(to_own), keep(from_first), keep(from_second), in_other, unread=1)
    collected = lax.all_to_all(summed, "zl", 0, 0, tiled=True)
    total = run(gathered_kernel, held(EXPERTS, CAP, COLS), 0, keep(collected))
    table = run(table_kernel, held(KEPT, TOK), 0, ids, total, unread=1)
    back = lax.all_to_all(total, ("zh", "x"), 0, 0, tiled=True)
    tokens_grad = run(combine_kernel, shape(TOK, COLS), 0, keep(table), keep(back))
    w_in_grad, w_out_grad = run(
        merge_kernel, (shape(*w_in.shape), shape(*w_out.shape)),
        0, keep(in_mine), keep(out_mine), keep(across(in_other)), keep(across(out_other)),
    )
    return tokens_grad, w_in_grad[None], w_out_grad[None]


def solution(mesh):
    fine = Mesh(mesh.devices.reshape(NY, NZ, NC, NH, NX), ("y", "zl", "c", "zh", "x"))
    dp, expert = ("y", "zl", "c"), ("zh", "x")
    placed = (
        P(expert, dp),
        P(expert, dp),
        P(expert, None),
        P(expert, None),
        P(expert, None, dp),
        P(expert, dp, None),
    )
    return jax.shard_map(
        on_device,
        mesh=fine,
        in_specs=placed,
        out_specs=(P(expert, dp), P(expert, None, dp), P(expert, dp, None)),
        check_vma=False,
    )
```

```python
import jax
import jax.numpy as jnp
from jax import lax
from jax.experimental import pallas as pl
from jax.experimental.pallas import tpu as pltpu
from jax.sharding import Mesh, PartitionSpec as P

NY, NZ, NC, NH, NX = 4, 4, 2, 4, 4
EXPERTS = NH * NX
TOK = 128
CAP = 20
MSG = 2 * CAP
COLS = 128
HID = 128
ROWS = EXPERTS * MSG
KEPT = EXPERTS * CAP
BF16 = jnp.bfloat16
F32 = jnp.float32
VMEM = pltpu.CompilerParams(vmem_limit_bytes=14 * 1024 * 1024)
CONTRACT_LAST = (((1,), (1,)), ((), ()))
CONTRACT_FIRST = (((0,), (0,)), ((), ()))


def slot_table(ids, rows_each, slot_of):
    experts = lax.broadcasted_iota(jnp.int32, (EXPERTS, TOK), 0)
    named = (experts == ids[0:1, :]) | (experts == ids[1:2, :])
    earlier = lax.broadcasted_iota(jnp.int32, (TOK, TOK), 0) < lax.broadcasted_iota(jnp.int32, (TOK, TOK), 1)
    prior = jnp.dot(named.astype(BF16), earlier.astype(BF16), preferred_element_type=F32)
    place = jnp.where(named, prior, -1.0).astype(BF16)
    shape = (EXPERTS, rows_each, TOK)
    expert = lax.broadcasted_iota(jnp.int32, shape, 0).reshape(EXPERTS * rows_each, TOK)
    row = lax.broadcasted_iota(jnp.int32, shape, 1).reshape(EXPERTS * rows_each, TOK)
    spread = (expert[:, :EXPERTS] == lax.broadcasted_iota(jnp.int32, (EXPERTS * rows_each, EXPERTS), 1)).astype(BF16)
    place_of_row = jnp.dot(spread, place, preferred_element_type=F32)
    return place_of_row == slot_of(row).astype(F32), expert, row


def dispatch_kernel(ids_ref, gate_ref, tok_ref, dy_ref, out_ref):
    ids = ids_ref[...]
    table, expert, row = slot_table(ids, MSG, lambda q: jnp.where(q >= CAP, q - CAP, q))
    gate = jnp.where(expert == ids[0:1, :], gate_ref[0:1, :], gate_ref[1:2, :])
    scale = jnp.sum(jnp.where(table, gate, 0.0), axis=1, keepdims=True)
    pick = table.astype(BF16)
    rows_in = jnp.dot(pick, tok_ref[...], preferred_element_type=F32)
    rows_dy = jnp.dot(pick, dy_ref[...], preferred_element_type=F32)
    out = jnp.where(row < CAP, rows_in, scale * rows_dy)
    out_ref[...] = out.astype(BF16).reshape(EXPERTS, MSG, COLS)


def split_kernel(w_in_ref, w_out_ref, after_ref, in_ref, out_ref, sems):
    del after_ref
    other = 1 - position()[1]
    blocks = NY * NZ
    copies = [pltpu.make_async_copy(w_in_ref.at[:, other], in_ref, sems.at[blocks])]
    for k in range(blocks):
        columns = pl.ds(pl.multiple_of((k * NC + other) * COLS, COLS), COLS)
        copies.append(pltpu.make_async_copy(w_out_ref.at[:, columns], out_ref.at[k], sems.at[k]))
    for copy in copies:
        copy.start()
    for copy in copies:
        copy.wait()


def table_kernel(ids_ref, after_ref, table_ref):
    del after_ref
    table, _, _ = slot_table(ids_ref[...], CAP, lambda q: q)
    table_ref[...] = table.astype(BF16)


def position():
    return lax.axis_index("y"), lax.axis_index("c")


def places(y, c):
    near, far = y + 1 - 2 * lax.rem(y, 2), NY - 1 - y
    return y, jnp.where(c == 0, near, far), jnp.where(c == 0, far, near), lax.rem(y + 2, NY)


def chunk(ref, zl):
    return ref[zl * EXPERTS:(zl + 1) * EXPERTS].reshape(ROWS, COLS)


def joined(first, second):
    return jnp.concatenate([first, second], axis=1)


def weights_in(w_in_ref, sib_ref, c, k):
    mine = w_in_ref[pl.ds(pl.multiple_of((k * NC + c) * COLS, COLS), COLS), :]
    return joined(mine, sib_ref[k])


def weights_out(w_out_ref, sib_ref, c, k):
    mine = w_out_ref[:, pl.ds(pl.multiple_of((k * NC + c) * COLS, COLS), COLS)]
    return jnp.concatenate([mine, sib_ref[k]], axis=0)


def forward(w_in_ref, w_out_ref, in_sib_ref, out_sib_ref, xs):
    _, c = position()
    at_of = places(position()[0], c)
    pre = jnp.zeros((ROWS, NC * HID), F32)
    act_grad = jnp.zeros((ROWS, NC * HID), F32)
    for place, blocks in xs:
        at = at_of[place] * NZ
        for zl in range(0, NZ, 2):
            x = joined(chunk(*blocks[zl]), chunk(*blocks[zl + 1]))
            w = jnp.concatenate([weights_in(w_in_ref, in_sib_ref, c, at + z) for z in (zl, zl + 1)], axis=0)
            v = joined(*[weights_out(w_out_ref, out_sib_ref, c, at + z) for z in (zl, zl + 1)])
            pre = pre + jnp.dot(x, w, preferred_element_type=F32)
            act_grad = act_grad + lax.dot_general(x, v, CONTRACT_LAST, preferred_element_type=F32)
    row = lax.broadcasted_iota(jnp.int32, (EXPERTS, MSG, NC * HID), 1).reshape(ROWS, NC * HID)
    return jnp.where(row < CAP, pre, act_grad)


def whole(ref):
    return [(ref, z) for z in range(NZ)]


def halves(low, high):
    return [(low, 0), (low, 1), (high, 0), (high, 1)]


def forward_first_kernel(wi, wo, wis, wos, own, first_a, first_b, out_ref):
    out_ref[...] = forward(wi, wo, wis, wos, [(0, whole(own)), (1, halves(first_a, first_b))])


def forward_second_kernel(wi, wo, wis, wos, second_a, second_b, before_ref, out_ref):
    out_ref[...] = before_ref[...] + forward(wi, wo, wis, wos, [(2, halves(second_a, second_b))])


def forward_last_kernel(wi, wo, wis, wos, last_a, last_b, before_ref, out_ref, sent_ref):
    total = before_ref[...] + forward(wi, wo, wis, wos, [(3, halves(last_a, last_b))])
    out_ref[...] = total
    sent_ref[...] = total.astype(BF16)


def activations(part_ref, part_sib_ref):
    passed = part_sib_ref[...]
    both = part_ref[...] + joined(passed[:, HID:], passed[:, :HID]).astype(F32)
    act_grad = jnp.concatenate([both[CAP:], both[:CAP]], axis=0)
    act, pullback = jax.vjp(lambda v: jax.nn.gelu(v, approximate=True), both)
    pre_grad = pullback(act_grad)[0]
    act = jnp.concatenate([act[ROWS - CAP:], act[:ROWS - CAP]], axis=0)
    row = lax.broadcasted_iota(jnp.int32, (EXPERTS, MSG, NC * HID), 1).reshape(ROWS, NC * HID)
    return jnp.where(row < CAP, pre_grad, 0.0).astype(BF16), jnp.where(row < CAP, 0.0, act).astype(BF16)


def middle_kernel(w_in_ref, sib_ref, part_ref, part_sib_ref, *outs):
    y, c = position()
    pre_grad, _ = activations(part_ref, part_sib_ref)
    block = lax.broadcasted_iota(jnp.int32, (EXPERTS, CAP, ROWS), 0).reshape(KEPT, ROWS)
    within = lax.broadcasted_iota(jnp.int32, (EXPERTS, CAP, ROWS), 1).reshape(KEPT, ROWS)
    keep = (lax.broadcasted_iota(jnp.int32, (KEPT, ROWS), 1) == block * MSG + within).astype(BF16)
    pg = jnp.dot(keep, pre_grad, preferred_element_type=F32).astype(BF16)
    for at, out_ref in zip(places(y, c), outs):
        for zl in range(0, NZ, 2):
            w = jnp.concatenate([weights_in(w_in_ref, sib_ref, c, at * NZ + z) for z in (zl, zl + 1)], axis=0)
            out = lax.dot_general(pg, w, CONTRACT_LAST, preferred_element_type=F32).astype(BF16)
            for j in range(2):
                out_ref[zl + j] = out[:, j * COLS:(j + 1) * COLS]


def relay_kernel(mine_ref, passed_ref, out_ref):
    out_ref[...] = (mine_ref[...].astype(F32) + passed_ref[...].astype(F32)).astype(BF16)


def total_kernel(mine_ref, first_ref, second_ref, after_ref, out_ref):
    del after_ref
    out_ref[...] = (mine_ref[...].astype(F32) + first_ref[...].astype(F32) + second_ref[...].astype(F32)).astype(BF16)


def gathered_kernel(parts_ref, out_ref):
    total = parts_ref[0].astype(F32)
    for zl in range(1, NZ):
        total = total + parts_ref[zl].astype(F32)
    out_ref[...] = total.reshape(EXPERTS, CAP, COLS).astype(BF16)


def grads_kernel(part_ref, part_sib_ref, *refs):
    xs, (in_mine, out_mine, in_other, out_other) = refs[:7], refs[8:]
    left = joined(*activations(part_ref, part_sib_ref)).T
    xs = [whole(xs[0])] + [halves(*xs[i:i + 2]) for i in (1, 3, 5)]
    for y, blocks in zip(places(*position()), xs):
        at = y * NZ
        for zl in range(0, NZ, 2):
            x = joined(chunk(*blocks[zl]), chunk(*blocks[zl + 1]))
            both = jnp.dot(left, x, preferred_element_type=F32).astype(BF16)
            for ref, first in ((in_mine, 0), (in_other, HID)):
                turned = both[first:first + HID].T
                ref[at + zl] = turned[:COLS]
                ref[at + zl + 1] = turned[COLS:]
            lanes = pl.ds(pl.multiple_of((at + zl) * COLS, 2 * COLS), 2 * COLS)
            out_mine[:, lanes] = both[2 * HID:3 * HID]
            for j in range(2):
                out_other[at + zl + j] = both[3 * HID:, j * COLS:(j + 1) * COLS]


def merge_kernel(in_mine, out_mine, in_sib, out_sib, w_in_grad_ref, w_out_grad_ref):
    _, c = position()
    blocks = NY * NZ
    for k in range(blocks):
        mine = pl.ds(pl.multiple_of((k * NC + c) * COLS, COLS), COLS)
        other = pl.ds(pl.multiple_of((k * NC + 1 - c) * COLS, COLS), COLS)
        w_in_grad_ref[mine, :] = in_mine[k]
        w_in_grad_ref[other, :] = in_sib[k]
        w_out_grad_ref[:, mine] = out_mine[:, k * COLS:(k + 1) * COLS]
        w_out_grad_ref[:, other] = out_sib[k]


def combine_kernel(table_ref, back_ref, out_ref):
    rows = back_ref[...].astype(F32).reshape(KEPT, COLS).astype(BF16)
    out_ref[...] = lax.dot_general(table_ref[...], rows, CONTRACT_FIRST, preferred_element_type=F32).astype(BF16)


SMEM = pl.BlockSpec(memory_space=pltpu.SMEM)
WHOLE = pl.BlockSpec(memory_space=pltpu.VMEM)
UNREAD = pl.BlockSpec(memory_space=pl.ANY)


def shape(*dims, kind=BF16):
    return jax.ShapeDtypeStruct(dims, kind)


def held(*dims, kind=BF16):
    return pltpu.VMEM(dims, kind)


def keep(value):
    return pltpu.with_memory_space_constraint(value, pltpu.VMEM)


def far(value):
    return pltpu.with_memory_space_constraint(value, pltpu.HBM)


def run(kernel, outs, scalars, *args, unread=0, scratch=()):
    specs = [SMEM] * scalars + [WHOLE] * (len(args) - scalars - unread) + [UNREAD] * unread
    out_specs = jax.tree.map(lambda _: WHOLE, outs)
    return pl.pallas_call(
        kernel, out_shape=outs, in_specs=specs, out_specs=out_specs, scratch_shapes=scratch, compiler_params=VMEM
    )(*args)


def partner(value, which):
    near, far = [i ^ 1 for i in range(NY)], [NY - 1 - i for i in range(NY)]
    to = [(near, far), (far, near)]
    return lax.ppermute(value, ("y", "c"), [(i * NC + c, to[c][which][i] * NC + c) for i in range(NY) for c in range(NC)])


def across(value):
    return lax.ppermute(value, "c", [(0, 1), (1, 0)])


def on_device(tokens, out_grad, expert_ids, gate_weights, w_in, w_out):
    ids, gate = far(expert_ids.T), far(gate_weights.T)
    w_in, w_out = w_in[0], w_out[0]
    blocks = NY * NZ
    half_in, half_out = held(blocks, COLS, HID), held(HID, blocks * COLS)
    send = run(dispatch_kernel, shape(EXPERTS, MSG, COLS), 0, ids, gate, far(tokens), far(out_grad))
    in_other, out_other = run(
        split_kernel, (half_in, half_in), 0, far(w_in.reshape(blocks, NC, COLS, HID)), far(w_out), send,
        unread=3, scratch=[pltpu.SemaphoreType.DMA((blocks + 1,))],
    )
    in_sib, out_sib = across(in_other), across(out_other)
    received = lax.all_to_all(send, ("zh", "x"), 0, 0, tiled=True)
    own = lax.all_gather(received, "zl", axis=0, tiled=True)
    own, in_sib, out_sib = lax.optimization_barrier((own, in_sib, out_sib))
    weights = (w_in, w_out, keep(in_sib), keep(out_sib))
    cut = NZ // 2 * EXPERTS
    low, high = own[:cut], own[cut:]
    first_a, second_b = partner(low, 0), partner(high, 1)
    first_b, second_a = partner(high, 0), partner(low, 1)
    last_a, last_b = partner(first_a, 1), partner(second_b, 0)
    xs = [keep(x) for x in (own, first_a, first_b, second_a, second_b, last_a, last_b)]
    part = held(ROWS, NC * HID, kind=F32)
    some = run(forward_first_kernel, part, 0, *weights, *xs[:3])
    more = run(forward_second_kernel, part, 0, *weights, *xs[3:5], keep(some))
    mine, sent = run(
        forward_last_kernel, (part, held(ROWS, NC * HID)), 0, *weights, *xs[5:], keep(more)
    )
    rows = held(NZ, KEPT, COLS)
    parts = keep(mine), keep(across(sent))
    to_own, to_first, to_second, to_last = run(
        middle_kernel, (rows, rows, rows, rows), 0, w_in, keep(in_sib), *parts
    )
    passed, from_second = partner(to_last, 1), partner(to_second, 1)
    relayed = run(relay_kernel, rows, 0, keep(to_first), keep(passed))
    from_first = partner(relayed, 0)
    in_mine, out_mine, in_other, out_other = run(
        grads_kernel, (half_in, half_out, half_in, half_in), 0, *parts, *xs, relayed, unread=1
    )
    summed = run(total_kernel, rows, 0, keep(to_own), keep(from_first), keep(from_second), in_other, unread=1)
    collected = lax.all_to_all(summed, "zl", 0, 0, tiled=True)
    total = run(gathered_kernel, held(EXPERTS, CAP, COLS), 0, keep(collected))
    table = run(table_kernel, held(KEPT, TOK), 0, ids, total, unread=1)
    back = lax.all_to_all(total, ("zh", "x"), 0, 0, tiled=True)
    tokens_grad = run(combine_kernel, shape(TOK, COLS), 0, keep(table), keep(back))
    w_in_grad, w_out_grad = run(
        merge_kernel, (shape(*w_in.shape), shape(*w_out.shape)),
        0, keep(in_mine), keep(out_mine), keep(across(in_other)), keep(across(out_other)),
    )
    return tokens_grad, w_in_grad[None], w_out_grad[None]


def solution(mesh):
    fine = Mesh(mesh.devices.reshape(NY, NZ, NC, NH, NX), ("y", "zl", "c", "zh", "x"))
    dp, expert = ("y", "zl", "c"), ("zh", "x")
    placed = (
        P(expert, dp),
        P(expert, dp),
        P(expert, None),
        P(expert, None),
        P(expert, None, dp),
        P(expert, dp, None),
    )
    return jax.shard_map(
        on_device,
        mesh=fine,
        in_specs=placed,
        out_specs=(P(expert, dp), P(expert, None, dp), P(expert, dp, None)),
        check_vma=False,
    )
```

```python
import jax
import jax.numpy as jnp
from jax import lax
from jax.experimental import pallas as pl
from jax.experimental.pallas import tpu as pltpu
from jax.sharding import Mesh, PartitionSpec as P

NY, NZ, NC, NH, NX = 4, 4, 2, 4, 4
EXPERTS = NH * NX
TOK = 128
CAP = 20
MSG = 2 * CAP
COLS = 128
HID = 128
ROWS = EXPERTS * MSG
KEPT = EXPERTS * CAP
BF16 = jnp.bfloat16
F32 = jnp.float32
VMEM = pltpu.CompilerParams(vmem_limit_bytes=14 * 1024 * 1024)
CONTRACT_LAST = (((1,), (1,)), ((), ()))
CONTRACT_FIRST = (((0,), (0,)), ((), ()))


def slot_table(ids, rows_each, slot_of):
    experts = lax.broadcasted_iota(jnp.int32, (EXPERTS, TOK), 0)
    named = (experts == ids[0:1, :]) | (experts == ids[1:2, :])
    earlier = lax.broadcasted_iota(jnp.int32, (TOK, TOK), 0) < lax.broadcasted_iota(jnp.int32, (TOK, TOK), 1)
    prior = jnp.dot(named.astype(BF16), earlier.astype(BF16), preferred_element_type=F32)
    place = jnp.where(named, prior, -1.0).astype(BF16)
    shape = (EXPERTS, rows_each, TOK)
    expert = lax.broadcasted_iota(jnp.int32, shape, 0).reshape(EXPERTS * rows_each, TOK)
    row = lax.broadcasted_iota(jnp.int32, shape, 1).reshape(EXPERTS * rows_each, TOK)
    spread = (expert[:, :EXPERTS] == lax.broadcasted_iota(jnp.int32, (EXPERTS * rows_each, EXPERTS), 1)).astype(BF16)
    place_of_row = jnp.dot(spread, place, preferred_element_type=F32)
    return place_of_row == slot_of(row).astype(F32), expert, row


def dispatch_kernel(ids_ref, gate_ref, tok_ref, dy_ref, out_ref):
    ids = ids_ref[...]
    experts = lax.broadcasted_iota(jnp.int32, (EXPERTS, TOK), 0)
    first, second = experts == ids[0:1, :], experts == ids[1:2, :]
    earlier = lax.broadcasted_iota(jnp.int32, (TOK, TOK), 0) < lax.broadcasted_iota(jnp.int32, (TOK, TOK), 1)
    prior = jnp.dot((first | second).astype(BF16), earlier.astype(BF16), preferred_element_type=F32)
    place = jnp.where(first | second, prior, -1.0)
    gate = jnp.where(first, gate_ref[0:1, :], gate_ref[1:2, :])
    shape = (EXPERTS, MSG, TOK)
    row = lax.broadcasted_iota(jnp.int32, shape, 1)
    slot = jnp.where(row >= CAP, row - CAP, row).astype(F32)
    table = jnp.broadcast_to(place[:, None, :], shape) == slot
    weight = jnp.where(table, jnp.broadcast_to(gate[:, None, :], shape), 0.0)
    scale = jnp.sum(weight, axis=2, keepdims=True).reshape(ROWS, 1)
    pick = jnp.where(table, 1.0, 0.0).reshape(ROWS, TOK).astype(BF16)
    rows_in = jnp.dot(pick, tok_ref[...], preferred_element_type=F32)
    rows_dy = jnp.dot(pick, dy_ref[...], preferred_element_type=F32)
    out = jnp.where(row.reshape(ROWS, COLS) < CAP, rows_in, scale * rows_dy)
    out_ref[...] = out.astype(BF16).reshape(EXPERTS, MSG, COLS)


def split_kernel(w_in_ref, w_out_ref, after_ref, in_ref, out_ref, sems):
    del after_ref
    other = 1 - position()[1]
    blocks = NY * NZ
    copies = [pltpu.make_async_copy(w_in_ref.at[:, other], in_ref, sems.at[blocks])]
    for k in range(blocks):
        columns = pl.ds(pl.multiple_of((k * NC + other) * COLS, COLS), COLS)
        copies.append(pltpu.make_async_copy(w_out_ref.at[:, columns], out_ref.at[k], sems.at[k]))
    for copy in copies:
        copy.start()
    for copy in copies:
        copy.wait()


def table_kernel(ids_ref, after_ref, table_ref):
    del after_ref
    table, _, _ = slot_table(ids_ref[...], CAP, lambda q: q)
    table_ref[...] = table.astype(BF16)


def position():
    return lax.axis_index("y"), lax.axis_index("c")


def places(y, c):
    near, far = y + 1 - 2 * lax.rem(y, 2), NY - 1 - y
    return y, jnp.where(c == 0, near, far), jnp.where(c == 0, far, near), lax.rem(y + 2, NY)


def chunk(ref, zl):
    return ref[zl * EXPERTS:(zl + 1) * EXPERTS].reshape(ROWS, COLS)


def joined(first, second):
    return jnp.concatenate([first, second], axis=1)


def weights_in(w_in_ref, sib_ref, c, k):
    mine = w_in_ref[pl.ds(pl.multiple_of((k * NC + c) * COLS, COLS), COLS), :]
    return joined(mine, sib_ref[k])


def weights_out(w_out_ref, sib_ref, c, k):
    mine = w_out_ref[:, pl.ds(pl.multiple_of((k * NC + c) * COLS, COLS), COLS)]
    return jnp.concatenate([mine, sib_ref[k]], axis=0)


def forward(w_in_ref, w_out_ref, in_sib_ref, out_sib_ref, xs):
    _, c = position()
    at_of = places(position()[0], c)
    pre = jnp.zeros((ROWS, NC * HID), F32)
    act_grad = jnp.zeros((ROWS, NC * HID), F32)
    for place, blocks in xs:
        at = at_of[place] * NZ
        for zl in range(0, NZ, 2):
            x = joined(chunk(*blocks[zl]), chunk(*blocks[zl + 1]))
            w = jnp.concatenate([weights_in(w_in_ref, in_sib_ref, c, at + z) for z in (zl, zl + 1)], axis=0)
            v = joined(*[weights_out(w_out_ref, out_sib_ref, c, at + z) for z in (zl, zl + 1)])
            pre = pre + jnp.dot(x, w, preferred_element_type=F32)
            act_grad = act_grad + lax.dot_general(x, v, CONTRACT_LAST, preferred_element_type=F32)
    row = lax.broadcasted_iota(jnp.int32, (EXPERTS, MSG, NC * HID), 1).reshape(ROWS, NC * HID)
    return jnp.where(row < CAP, pre, act_grad)


def whole(ref):
    return [(ref, z) for z in range(NZ)]


def halves(low, high):
    return [(low, 0), (low, 1), (high, 0), (high, 1)]


def forward_first_kernel(wi, wo, wis, wos, own, first_a, first_b, out_ref):
    out_ref[...] = forward(wi, wo, wis, wos, [(0, whole(own)), (1, halves(first_a, first_b))])


def forward_second_kernel(wi, wo, wis, wos, second_a, second_b, before_ref, out_ref):
    out_ref[...] = before_ref[...] + forward(wi, wo, wis, wos, [(2, halves(second_a, second_b))])


def forward_last_kernel(wi, wo, wis, wos, last_a, last_b, before_ref, out_ref, sent_ref):
    total = before_ref[...] + forward(wi, wo, wis, wos, [(3, halves(last_a, last_b))])
    out_ref[...] = total
    sent_ref[...] = total.astype(BF16)


def activations(part_ref, part_sib_ref):
    passed = part_sib_ref[...]
    both = part_ref[...] + joined(passed[:, HID:], passed[:, :HID]).astype(F32)
    act_grad = jnp.concatenate([both[CAP:], both[:CAP]], axis=0)
    act, pullback = jax.vjp(lambda v: jax.nn.gelu(v, approximate=True), both)
    pre_grad = pullback(act_grad)[0]
    act = jnp.concatenate([act[ROWS - CAP:], act[:ROWS - CAP]], axis=0)
    row = lax.broadcasted_iota(jnp.int32, (EXPERTS, MSG, NC * HID), 1).reshape(ROWS, NC * HID)
    return jnp.where(row < CAP, pre_grad, 0.0).astype(BF16), jnp.where(row < CAP, 0.0, act).astype(BF16)


def partials(w_in_ref, sib_ref, pg, at, out_ref):
    _, c = position()
    for zl in range(0, NZ, 2):
        w = jnp.concatenate([weights_in(w_in_ref, sib_ref, c, at * NZ + z) for z in (zl, zl + 1)], axis=0)
        out = lax.dot_general(pg, w, CONTRACT_LAST, preferred_element_type=F32).astype(BF16)
        for j in range(2):
            out_ref[zl + j] = out[:, j * COLS:(j + 1) * COLS]


def far_kernel(w_in_ref, sib_ref, part_ref, part_sib_ref, pg_ref, out_ref):
    pre_grad, _ = activations(part_ref, part_sib_ref)
    block = lax.broadcasted_iota(jnp.int32, (EXPERTS, CAP, ROWS), 0).reshape(KEPT, ROWS)
    within = lax.broadcasted_iota(jnp.int32, (EXPERTS, CAP, ROWS), 1).reshape(KEPT, ROWS)
    keep = (lax.broadcasted_iota(jnp.int32, (KEPT, ROWS), 1) == block * MSG + within).astype(BF16)
    pg = jnp.dot(keep, pre_grad, preferred_element_type=F32).astype(BF16)
    pg_ref[...] = pg
    partials(w_in_ref, sib_ref, pg, places(*position())[3], out_ref)


def near_kernel(w_in_ref, sib_ref, pg_ref, *outs):
    pg = pg_ref[...]
    for at, out_ref in zip(places(*position()), outs):
        partials(w_in_ref, sib_ref, pg, at, out_ref)


def relay_kernel(mine_ref, passed_ref, out_ref):
    out_ref[...] = (mine_ref[...].astype(F32) + passed_ref[...].astype(F32)).astype(BF16)


def total_kernel(mine_ref, first_ref, second_ref, after_ref, out_ref):
    del after_ref
    out_ref[...] = (mine_ref[...].astype(F32) + first_ref[...].astype(F32) + second_ref[...].astype(F32)).astype(BF16)


def gathered_kernel(parts_ref, out_ref):
    total = parts_ref[0].astype(F32)
    for zl in range(1, NZ):
        total = total + parts_ref[zl].astype(F32)
    out_ref[...] = total.reshape(EXPERTS, CAP, COLS).astype(BF16)


def grads_kernel(part_ref, part_sib_ref, *refs):
    xs, (in_mine, out_mine, in_other, out_other) = refs[:7], refs[8:]
    left = joined(*activations(part_ref, part_sib_ref)).T
    xs = [whole(xs[0])] + [halves(*xs[i:i + 2]) for i in (1, 3, 5)]
    for y, blocks in zip(places(*position()), xs):
        at = y * NZ
        for zl in range(0, NZ, 2):
            x = joined(chunk(*blocks[zl]), chunk(*blocks[zl + 1]))
            both = jnp.dot(left, x, preferred_element_type=F32).astype(BF16)
            for ref, first in ((in_mine, 0), (in_other, HID)):
                turned = both[first:first + HID].T
                ref[at + zl] = turned[:COLS]
                ref[at + zl + 1] = turned[COLS:]
            lanes = pl.ds(pl.multiple_of((at + zl) * COLS, 2 * COLS), 2 * COLS)
            out_mine[:, lanes] = both[2 * HID:3 * HID]
            for j in range(2):
                out_other[at + zl + j] = both[3 * HID:, j * COLS:(j + 1) * COLS]


def merge_kernel(in_mine, out_mine, in_sib, out_sib, w_in_grad_ref, w_out_grad_ref):
    _, c = position()
    blocks = NY * NZ
    for k in range(blocks):
        mine = pl.ds(pl.multiple_of((k * NC + c) * COLS, COLS), COLS)
        other = pl.ds(pl.multiple_of((k * NC + 1 - c) * COLS, COLS), COLS)
        w_in_grad_ref[mine, :] = in_mine[k]
        w_in_grad_ref[other, :] = in_sib[k]
        w_out_grad_ref[:, mine] = out_mine[:, k * COLS:(k + 1) * COLS]
        w_out_grad_ref[:, other] = out_sib[k]


def combine_kernel(table_ref, back_ref, out_ref):
    rows = back_ref[...].astype(F32).reshape(KEPT, COLS).astype(BF16)
    out_ref[...] = lax.dot_general(table_ref[...], rows, CONTRACT_FIRST, preferred_element_type=F32).astype(BF16)


SMEM = pl.BlockSpec(memory_space=pltpu.SMEM)
WHOLE = pl.BlockSpec(memory_space=pltpu.VMEM)
UNREAD = pl.BlockSpec(memory_space=pl.ANY)


def shape(*dims, kind=BF16):
    return jax.ShapeDtypeStruct(dims, kind)


def held(*dims, kind=BF16):
    return pltpu.VMEM(dims, kind)


def keep(value):
    return pltpu.with_memory_space_constraint(value, pltpu.VMEM)


def far(value):
    return pltpu.with_memory_space_constraint(value, pltpu.HBM)


def run(kernel, outs, scalars, *args, unread=0, scratch=()):
    specs = [SMEM] * scalars + [WHOLE] * (len(args) - scalars - unread) + [UNREAD] * unread
    out_specs = jax.tree.map(lambda _: WHOLE, outs)
    return pl.pallas_call(
        kernel, out_shape=outs, in_specs=specs, out_specs=out_specs, scratch_shapes=scratch, compiler_params=VMEM
    )(*args)


def partner(value, which):
    near, far = [i ^ 1 for i in range(NY)], [NY - 1 - i for i in range(NY)]
    to = [(near, far), (far, near)]
    return lax.ppermute(value, ("y", "c"), [(i * NC + c, to[c][which][i] * NC + c) for i in range(NY) for c in range(NC)])


def across(value):
    return lax.ppermute(value, "c", [(0, 1), (1, 0)])


def on_device(tokens, out_grad, expert_ids, gate_weights, w_in, w_out):
    ids, gate = far(expert_ids.T), far(gate_weights.T)
    w_in, w_out = w_in[0], w_out[0]
    blocks = NY * NZ
    half_in, half_out = held(blocks, COLS, HID), held(HID, blocks * COLS)
    send = run(dispatch_kernel, shape(EXPERTS, MSG, COLS), 0, ids, gate, far(tokens), far(out_grad))
    in_other, out_other = run(
        split_kernel, (half_in, half_in), 0, far(w_in.reshape(blocks, NC, COLS, HID)), far(w_out), send,
        unread=3, scratch=[pltpu.SemaphoreType.DMA((blocks + 1,))],
    )
    in_sib, out_sib = across(in_other), across(out_other)
    received = lax.all_to_all(send, ("zh", "x"), 0, 0, tiled=True)
    own = lax.all_gather(received, "zl", axis=0, tiled=True)
    own, in_sib, out_sib = lax.optimization_barrier((own, in_sib, out_sib))
    weights = (w_in, w_out, keep(in_sib), keep(out_sib))
    cut = NZ // 2 * EXPERTS
    low, high = own[:cut], own[cut:]
    first_a, second_b = partner(low, 0), partner(high, 1)
    first_b, second_a = partner(high, 0), partner(low, 1)
    last_a, last_b = partner(first_a, 1), partner(second_b, 0)
    xs = [keep(x) for x in (own, first_a, first_b, second_a, second_b, last_a, last_b)]
    part = held(ROWS, NC * HID, kind=F32)
    some = run(forward_first_kernel, part, 0, *weights, *xs[:3])
    more = run(forward_second_kernel, part, 0, *weights, *xs[3:5], keep(some))
    mine, sent = run(
        forward_last_kernel, (part, held(ROWS, NC * HID)), 0, *weights, *xs[5:], keep(more)
    )
    rows = held(NZ, KEPT, COLS)
    parts = keep(mine), keep(across(sent))
    pg, to_last = run(far_kernel, (held(KEPT, NC * HID), rows), 0, w_in, keep(in_sib), *parts)
    to_own, to_first, to_second = run(near_kernel, (rows, rows, rows), 0, w_in, keep(in_sib), keep(pg))
    passed, from_second = partner(to_last, 1), partner(to_second, 1)
    relayed = run(relay_kernel, rows, 0, keep(to_first), keep(passed))
    from_first = partner(relayed, 0)
    in_mine, out_mine, in_other, out_other = run(
        grads_kernel, (half_in, half_out, half_in, half_in), 0, *parts, *xs, relayed, unread=1
    )
    summed = run(total_kernel, rows, 0, keep(to_own), keep(from_first), keep(from_second), in_other, unread=1)
    collected = lax.all_to_all(summed, "zl", 0, 0, tiled=True)
    total = run(gathered_kernel, held(EXPERTS, CAP, COLS), 0, keep(collected))
    table = run(table_kernel, held(KEPT, TOK), 0, ids, total, unread=1)
    back = lax.all_to_all(total, ("zh", "x"), 0, 0, tiled=True)
    tokens_grad = run(combine_kernel, shape(TOK, COLS), 0, keep(table), keep(back))
    w_in_grad, w_out_grad = run(
        merge_kernel, (shape(*w_in.shape), shape(*w_out.shape)),
        0, keep(in_mine), keep(out_mine), keep(across(in_other)), keep(across(out_other)),
    )
    return tokens_grad, w_in_grad[None], w_out_grad[None]


def solution(mesh):
    fine = Mesh(mesh.devices.reshape(NY, NZ, NC, NH, NX), ("y", "zl", "c", "zh", "x"))
    dp, expert = ("y", "zl", "c"), ("zh", "x")
    placed = (
        P(expert, dp),
        P(expert, dp),
        P(expert, None),
        P(expert, None),
        P(expert, None, dp),
        P(expert, dp, None),
    )
    return jax.shard_map(
        on_device,
        mesh=fine,
        in_specs=placed,
        out_specs=(P(expert, dp), P(expert, None, dp), P(expert, dp, None)),
        check_vma=False,
    )
```

```python
import jax
import jax.numpy as jnp
from jax import lax
from jax.experimental import pallas as pl
from jax.experimental.pallas import tpu as pltpu
from jax.sharding import Mesh, PartitionSpec as P

NY, NZ, NC, NH, NX = 4, 4, 2, 4, 4
EXPERTS = NH * NX
TOK = 128
CAP = 20
MSG = 2 * CAP
COLS = 128
HID = 128
ROWS = EXPERTS * MSG
KEPT = EXPERTS * CAP
BF16 = jnp.bfloat16
F32 = jnp.float32
VMEM = pltpu.CompilerParams(vmem_limit_bytes=14 * 1024 * 1024)
CONTRACT_LAST = (((1,), (1,)), ((), ()))


def slot_table(ids, rows_each, slot_of):
    experts = lax.broadcasted_iota(jnp.int32, (EXPERTS, TOK), 0)
    named = (experts == ids[0:1, :]) | (experts == ids[1:2, :])
    earlier = lax.broadcasted_iota(jnp.int32, (TOK, TOK), 0) < lax.broadcasted_iota(jnp.int32, (TOK, TOK), 1)
    prior = jnp.dot(named.astype(BF16), earlier.astype(BF16), preferred_element_type=F32)
    place = jnp.where(named, prior, -1.0).astype(BF16)
    shape = (EXPERTS, rows_each, TOK)
    expert = lax.broadcasted_iota(jnp.int32, shape, 0).reshape(EXPERTS * rows_each, TOK)
    row = lax.broadcasted_iota(jnp.int32, shape, 1).reshape(EXPERTS * rows_each, TOK)
    spread = (expert[:, :EXPERTS] == lax.broadcasted_iota(jnp.int32, (EXPERTS * rows_each, EXPERTS), 1)).astype(BF16)
    place_of_row = jnp.dot(spread, place, preferred_element_type=F32)
    return place_of_row == slot_of(row).astype(F32), expert, row


def dispatch_kernel(ids_ref, gate_ref, tok_ref, dy_ref, out_ref):
    ids = ids_ref[...]
    experts = lax.broadcasted_iota(jnp.int32, (EXPERTS, TOK), 0)
    first, second = experts == ids[0:1, :], experts == ids[1:2, :]
    earlier = lax.broadcasted_iota(jnp.int32, (TOK, TOK), 0) < lax.broadcasted_iota(jnp.int32, (TOK, TOK), 1)
    prior = jnp.dot((first | second).astype(BF16), earlier.astype(BF16), preferred_element_type=F32)
    place = jnp.where(first | second, prior, -1.0)
    gate = jnp.where(first, gate_ref[0:1, :], gate_ref[1:2, :])
    shape = (EXPERTS, MSG, TOK)
    row = lax.broadcasted_iota(jnp.int32, shape, 1)
    slot = jnp.where(row >= CAP, row - CAP, row).astype(F32)
    table = jnp.broadcast_to(place[:, None, :], shape) == slot
    weight = jnp.where(table, jnp.broadcast_to(gate[:, None, :], shape), 0.0)
    scale = jnp.sum(weight, axis=2, keepdims=True).reshape(ROWS, 1)
    pick = jnp.where(table, 1.0, 0.0).reshape(ROWS, TOK).astype(BF16)
    rows_in = jnp.dot(pick, tok_ref[...], preferred_element_type=F32)
    rows_dy = jnp.dot(pick, dy_ref[...], preferred_element_type=F32)
    out = jnp.where(row.reshape(ROWS, COLS) < CAP, rows_in, scale * rows_dy)
    out_ref[...] = out.astype(BF16).reshape(EXPERTS, MSG, COLS)


def split_kernel(w_in_ref, w_out_ref, after_ref, in_ref, out_ref, sems):
    del after_ref
    other = 1 - position()[1]
    blocks = NY * NZ
    copies = [pltpu.make_async_copy(w_in_ref.at[:, other], in_ref, sems.at[blocks])]
    for k in range(blocks):
        columns = pl.ds(pl.multiple_of((k * NC + other) * COLS, COLS), COLS)
        copies.append(pltpu.make_async_copy(w_out_ref.at[:, columns], out_ref.at[k], sems.at[k]))
    for copy in copies:
        copy.start()
    for copy in copies:
        copy.wait()


def table_kernel(ids_ref, after_ref, table_ref):
    del after_ref
    table, _, _ = slot_table(ids_ref[...], CAP, lambda q: q)
    table_ref[...] = table.astype(BF16).T


def position():
    return lax.axis_index("y"), lax.axis_index("c")


def places(y, c):
    near, far = y + 1 - 2 * lax.rem(y, 2), NY - 1 - y
    return y, jnp.where(c == 0, near, far), jnp.where(c == 0, far, near), lax.rem(y + 2, NY)


def chunk(ref, zl):
    return ref[zl * EXPERTS:(zl + 1) * EXPERTS].reshape(ROWS, COLS)


def joined(first, second):
    return jnp.concatenate([first, second], axis=1)


def weights_in(w_in_ref, sib_ref, c, k):
    mine = w_in_ref[pl.ds(pl.multiple_of((k * NC + c) * COLS, COLS), COLS), :]
    return joined(mine, sib_ref[k])


def weights_out(w_out_ref, sib_ref, c, k):
    mine = w_out_ref[:, pl.ds(pl.multiple_of((k * NC + c) * COLS, COLS), COLS)]
    return jnp.concatenate([mine, sib_ref[k]], axis=0)


def forward(w_in_ref, w_out_ref, in_sib_ref, out_sib_ref, xs):
    _, c = position()
    at_of = places(position()[0], c)
    pre = jnp.zeros((ROWS, NC * HID), F32)
    act_grad = jnp.zeros((ROWS, NC * HID), F32)
    for place, blocks in xs:
        at = at_of[place] * NZ
        for zl in range(0, NZ, 2):
            x = joined(chunk(*blocks[zl]), chunk(*blocks[zl + 1]))
            w = jnp.concatenate([weights_in(w_in_ref, in_sib_ref, c, at + z) for z in (zl, zl + 1)], axis=0)
            v = joined(*[weights_out(w_out_ref, out_sib_ref, c, at + z) for z in (zl, zl + 1)])
            pre = pre + jnp.dot(x, w, preferred_element_type=F32)
            act_grad = act_grad + lax.dot_general(x, v, CONTRACT_LAST, preferred_element_type=F32)
    row = lax.broadcasted_iota(jnp.int32, (EXPERTS, MSG, NC * HID), 1).reshape(ROWS, NC * HID)
    return jnp.where(row < CAP, pre, act_grad)


def whole(ref):
    return [(ref, z) for z in range(NZ)]


def halves(low, high):
    return [(low, 0), (low, 1), (high, 0), (high, 1)]


def forward_first_kernel(wi, wo, wis, wos, own, first_a, first_b, out_ref):
    out_ref[...] = forward(wi, wo, wis, wos, [(0, whole(own)), (1, halves(first_a, first_b))])


def forward_second_kernel(wi, wo, wis, wos, second_a, second_b, before_ref, out_ref):
    out_ref[...] = before_ref[...] + forward(wi, wo, wis, wos, [(2, halves(second_a, second_b))])


def forward_last_kernel(wi, wo, wis, wos, last_a, last_b, before_ref, out_ref, sent_ref):
    total = before_ref[...] + forward(wi, wo, wis, wos, [(3, halves(last_a, last_b))])
    out_ref[...] = total
    sent_ref[...] = total.astype(BF16)


def activations(part_ref, part_sib_ref):
    passed = part_sib_ref[...]
    both = part_ref[...] + joined(passed[:, HID:], passed[:, :HID]).astype(F32)
    act_grad = jnp.concatenate([both[CAP:], both[:CAP]], axis=0)
    act, pullback = jax.vjp(lambda v: jax.nn.gelu(v, approximate=True), both)
    pre_grad = pullback(act_grad)[0]
    act = jnp.concatenate([act[ROWS - CAP:], act[:ROWS - CAP]], axis=0)
    row = lax.broadcasted_iota(jnp.int32, (EXPERTS, MSG, NC * HID), 1).reshape(ROWS, NC * HID)
    return jnp.where(row < CAP, pre_grad, 0.0).astype(BF16), jnp.where(row < CAP, 0.0, act).astype(BF16)


def partials(w_in_ref, sib_ref, pg, at, out_ref):
    _, c = position()
    for zl in range(0, NZ, 2):
        w = jnp.concatenate([weights_in(w_in_ref, sib_ref, c, at * NZ + z) for z in (zl, zl + 1)], axis=0)
        out = lax.dot_general(pg, w, CONTRACT_LAST, preferred_element_type=F32).astype(BF16)
        for j in range(2):
            out_ref[zl + j] = out[:, j * COLS:(j + 1) * COLS]


def far_kernel(w_in_ref, sib_ref, part_ref, part_sib_ref, pg_ref, out_ref):
    pre_grad, _ = activations(part_ref, part_sib_ref)
    pg = pre_grad.astype(F32).reshape(EXPERTS, MSG, NC * HID)[:, :CAP].reshape(KEPT, NC * HID).astype(BF16)
    pg_ref[...] = pg
    partials(w_in_ref, sib_ref, pg, places(*position())[3], out_ref)


def near_kernel(w_in_ref, sib_ref, pg_ref, *outs):
    pg = pg_ref[...]
    for at, out_ref in zip(places(*position()), outs):
        partials(w_in_ref, sib_ref, pg, at, out_ref)


def relay_kernel(mine_ref, passed_ref, out_ref):
    out_ref[...] = (mine_ref[...].astype(F32) + passed_ref[...].astype(F32)).astype(BF16)


def total_kernel(mine_ref, first_ref, second_ref, after_ref, out_ref):
    del after_ref
    out_ref[...] = (mine_ref[...].astype(F32) + first_ref[...].astype(F32) + second_ref[...].astype(F32)).astype(BF16)


def gathered_kernel(parts_ref, out_ref):
    total = parts_ref[0].astype(F32)
    for zl in range(1, NZ):
        total = total + parts_ref[zl].astype(F32)
    out_ref[...] = total.reshape(EXPERTS, CAP, COLS).astype(BF16)


def grads_kernel(part_ref, part_sib_ref, *refs):
    xs, (in_mine, out_mine, in_other, out_other) = refs[:7], refs[8:]
    left = joined(*activations(part_ref, part_sib_ref)).T
    xs = [whole(xs[0])] + [halves(*xs[i:i + 2]) for i in (1, 3, 5)]
    for y, blocks in zip(places(*position()), xs):
        at = y * NZ
        for zl in range(0, NZ, 2):
            x = joined(chunk(*blocks[zl]), chunk(*blocks[zl + 1]))
            both = jnp.dot(left, x, preferred_element_type=F32).astype(BF16)
            for ref, first in ((in_mine, 0), (in_other, HID)):
                turned = both[first:first + HID].T
                ref[at + zl] = turned[:COLS]
                ref[at + zl + 1] = turned[COLS:]
            lanes = pl.ds(pl.multiple_of((at + zl) * COLS, 2 * COLS), 2 * COLS)
            out_mine[:, lanes] = both[2 * HID:3 * HID]
            for j in range(2):
                out_other[at + zl + j] = both[3 * HID:, j * COLS:(j + 1) * COLS]


def merge_kernel(in_mine, out_mine, in_sib, out_sib, w_in_grad_ref, w_out_grad_ref):
    _, c = position()
    blocks = NY * NZ
    for k in range(blocks):
        mine = pl.ds(pl.multiple_of((k * NC + c) * COLS, COLS), COLS)
        other = pl.ds(pl.multiple_of((k * NC + 1 - c) * COLS, COLS), COLS)
        w_in_grad_ref[mine, :] = in_mine[k]
        w_in_grad_ref[other, :] = in_sib[k]
        w_out_grad_ref[:, mine] = out_mine[:, k * COLS:(k + 1) * COLS]
        w_out_grad_ref[:, other] = out_sib[k]


def combine_kernel(table_ref, back_ref, out_ref):
    rows = back_ref[...].astype(F32).reshape(KEPT, COLS).astype(BF16)
    out_ref[...] = jnp.dot(table_ref[...], rows, preferred_element_type=F32).astype(BF16)


SMEM = pl.BlockSpec(memory_space=pltpu.SMEM)
WHOLE = pl.BlockSpec(memory_space=pltpu.VMEM)
UNREAD = pl.BlockSpec(memory_space=pl.ANY)


def shape(*dims, kind=BF16):
    return jax.ShapeDtypeStruct(dims, kind)


def held(*dims, kind=BF16):
    return pltpu.VMEM(dims, kind)


def keep(value):
    return pltpu.with_memory_space_constraint(value, pltpu.VMEM)


def far(value):
    return pltpu.with_memory_space_constraint(value, pltpu.HBM)


def run(kernel, outs, scalars, *args, unread=0, scratch=()):
    specs = [SMEM] * scalars + [WHOLE] * (len(args) - scalars - unread) + [UNREAD] * unread
    out_specs = jax.tree.map(lambda _: WHOLE, outs)
    return pl.pallas_call(
        kernel, out_shape=outs, in_specs=specs, out_specs=out_specs, scratch_shapes=scratch, compiler_params=VMEM
    )(*args)


def partner(value, which):
    near, far = [i ^ 1 for i in range(NY)], [NY - 1 - i for i in range(NY)]
    to = [(near, far), (far, near)]
    return lax.ppermute(value, ("y", "c"), [(i * NC + c, to[c][which][i] * NC + c) for i in range(NY) for c in range(NC)])


def across(value):
    return lax.ppermute(value, "c", [(0, 1), (1, 0)])


def on_device(tokens, out_grad, expert_ids, gate_weights, w_in, w_out):
    ids, gate = far(expert_ids.T), far(gate_weights.T)
    w_in, w_out = w_in[0], w_out[0]
    blocks = NY * NZ
    half_in, half_out = held(blocks, COLS, HID), held(HID, blocks * COLS)
    send = run(dispatch_kernel, shape(EXPERTS, MSG, COLS), 0, ids, gate, far(tokens), far(out_grad))
    in_other, out_other = run(
        split_kernel, (half_in, half_in), 0, far(w_in.reshape(blocks, NC, COLS, HID)), far(w_out), send,
        unread=3, scratch=[pltpu.SemaphoreType.DMA((blocks + 1,))],
    )
    in_sib, out_sib = across(in_other), across(out_other)
    received = lax.all_to_all(send, ("zh", "x"), 0, 0, tiled=True)
    own = lax.all_gather(received, "zl", axis=0, tiled=True)
    own, in_sib, out_sib = lax.optimization_barrier((own, in_sib, out_sib))
    weights = (w_in, w_out, keep(in_sib), keep(out_sib))
    cut = NZ // 2 * EXPERTS
    low, high = own[:cut], own[cut:]
    first_a, second_b = partner(low, 0), partner(high, 1)
    first_b, second_a = partner(high, 0), partner(low, 1)
    last_a, last_b = partner(first_a, 1), partner(second_b, 0)
    xs = [keep(x) for x in (own, first_a, first_b, second_a, second_b, last_a, last_b)]
    part = held(ROWS, NC * HID, kind=F32)
    some = run(forward_first_kernel, part, 0, *weights, *xs[:3])
    more = run(forward_second_kernel, part, 0, *weights, *xs[3:5], keep(some))
    mine, sent = run(
        forward_last_kernel, (part, held(ROWS, NC * HID)), 0, *weights, *xs[5:], keep(more)
    )
    rows = held(NZ, KEPT, COLS)
    parts = keep(mine), keep(across(sent))
    pg, to_last = run(far_kernel, (held(KEPT, NC * HID), rows), 0, w_in, keep(in_sib), *parts)
    to_own, to_first, to_second = run(near_kernel, (rows, rows, rows), 0, w_in, keep(in_sib), keep(pg))
    passed, from_second = partner(to_last, 1), partner(to_second, 1)
    relayed = run(relay_kernel, rows, 0, keep(to_first), keep(passed))
    from_first = partner(relayed, 0)
    in_mine, out_mine, in_other, out_other = run(
        grads_kernel, (half_in, half_out, half_in, half_in), 0, *parts, *xs, relayed, unread=1
    )
    summed = run(total_kernel, rows, 0, keep(to_own), keep(from_first), keep(from_second), in_other, unread=1)
    collected = lax.all_to_all(summed, "zl", 0, 0, tiled=True)
    total = run(gathered_kernel, held(EXPERTS, CAP, COLS), 0, keep(collected))
    table = run(table_kernel, held(TOK, KEPT), 0, ids, total, unread=1)
    back = lax.all_to_all(total, ("zh", "x"), 0, 0, tiled=True)
    tokens_grad = run(combine_kernel, shape(TOK, COLS), 0, keep(table), keep(back))
    w_in_grad, w_out_grad = run(
        merge_kernel, (shape(*w_in.shape), shape(*w_out.shape)),
        0, keep(in_mine), keep(out_mine), keep(across(in_other)), keep(across(out_other)),
    )
    return tokens_grad, w_in_grad[None], w_out_grad[None]


def solution(mesh):
    fine = Mesh(mesh.devices.reshape(NY, NZ, NC, NH, NX), ("y", "zl", "c", "zh", "x"))
    dp, expert = ("y", "zl", "c"), ("zh", "x")
    placed = (
        P(expert, dp),
        P(expert, dp),
        P(expert, None),
        P(expert, None),
        P(expert, None, dp),
        P(expert, dp, None),
    )
    return jax.shard_map(
        on_device,
        mesh=fine,
        in_specs=placed,
        out_specs=(P(expert, dp), P(expert, None, dp), P(expert, dp, None)),
        check_vma=False,
    )
```

```python
import jax
import jax.numpy as jnp
from jax import lax
from jax.experimental import pallas as pl
from jax.experimental.pallas import tpu as pltpu
from jax.sharding import Mesh, PartitionSpec as P

NY, NZ, NC, NH, NX = 4, 4, 2, 4, 4
EXPERTS = NH * NX
TOK = 128
CAP = 20
MSG = 2 * CAP
COLS = 128
HID = 128
ROWS = EXPERTS * MSG
KEPT = EXPERTS * CAP
BF16 = jnp.bfloat16
F32 = jnp.float32
VMEM = pltpu.CompilerParams(vmem_limit_bytes=14 * 1024 * 1024)
CONTRACT_LAST = (((1,), (1,)), ((), ()))


def slot_table(ids, rows_each, slot_of):
    experts = lax.broadcasted_iota(jnp.int32, (EXPERTS, TOK), 0)
    named = (experts == ids[0:1, :]) | (experts == ids[1:2, :])
    earlier = lax.broadcasted_iota(jnp.int32, (TOK, TOK), 0) < lax.broadcasted_iota(jnp.int32, (TOK, TOK), 1)
    prior = jnp.dot(named.astype(BF16), earlier.astype(BF16), preferred_element_type=F32)
    place = jnp.where(named, prior, -1.0).astype(BF16)
    shape = (EXPERTS, rows_each, TOK)
    expert = lax.broadcasted_iota(jnp.int32, shape, 0).reshape(EXPERTS * rows_each, TOK)
    row = lax.broadcasted_iota(jnp.int32, shape, 1).reshape(EXPERTS * rows_each, TOK)
    spread = (expert[:, :EXPERTS] == lax.broadcasted_iota(jnp.int32, (EXPERTS * rows_each, EXPERTS), 1)).astype(BF16)
    place_of_row = jnp.dot(spread, place, preferred_element_type=F32)
    return place_of_row == slot_of(row).astype(F32), expert, row


def dispatch_kernel(ids_ref, gate_ref, tok_ref, dy_ref, out_ref):
    ids = ids_ref[...]
    experts = lax.broadcasted_iota(jnp.int32, (EXPERTS, TOK), 0)
    first, second = experts == ids[0:1, :], experts == ids[1:2, :]
    earlier = lax.broadcasted_iota(jnp.int32, (TOK, TOK), 0) < lax.broadcasted_iota(jnp.int32, (TOK, TOK), 1)
    prior = jnp.dot((first | second).astype(BF16), earlier.astype(BF16), preferred_element_type=F32)
    place = jnp.where(first | second, prior, -1.0)
    gate = jnp.where(first, gate_ref[0:1, :], gate_ref[1:2, :])
    shape = (EXPERTS, MSG, TOK)
    row = lax.broadcasted_iota(jnp.int32, shape, 1)
    slot = jnp.where(row >= CAP, row - CAP, row).astype(F32)
    table = jnp.broadcast_to(place[:, None, :], shape) == slot
    weight = jnp.where(table, jnp.broadcast_to(gate[:, None, :], shape), 0.0)
    scale = jnp.sum(weight, axis=2, keepdims=True).reshape(ROWS, 1)
    is_in = row.reshape(ROWS, TOK) < CAP
    pick = jnp.where(table, 1.0, 0.0).reshape(ROWS, TOK)
    pick = joined(jnp.where(is_in, pick, 0.0), jnp.where(is_in, 0.0, pick)).astype(BF16)
    source = jnp.concatenate([tok_ref[...], dy_ref[...]], axis=0)
    out = jnp.dot(pick, source, preferred_element_type=F32)
    out = jnp.where(is_in, out, scale * out)
    out_ref[...] = out.astype(BF16).reshape(EXPERTS, MSG, COLS)


def split_kernel(w_in_ref, w_out_ref, after_ref, in_ref, out_ref, sems):
    del after_ref
    other = 1 - position()[1]
    blocks = NY * NZ
    copies = [pltpu.make_async_copy(w_in_ref.at[:, other], in_ref, sems.at[blocks])]
    for k in range(blocks):
        columns = pl.ds(pl.multiple_of((k * NC + other) * COLS, COLS), COLS)
        copies.append(pltpu.make_async_copy(w_out_ref.at[:, columns], out_ref.at[k], sems.at[k]))
    for copy in copies:
        copy.start()
    for copy in copies:
        copy.wait()


def table_kernel(ids_ref, after_ref, table_ref):
    del after_ref
    table, _, _ = slot_table(ids_ref[...], CAP, lambda q: q)
    table_ref[...] = table.astype(BF16).T


def position():
    return lax.axis_index("y"), lax.axis_index("c")


def places(y, c):
    near, far = y + 1 - 2 * lax.rem(y, 2), NY - 1 - y
    return y, jnp.where(c == 0, near, far), jnp.where(c == 0, far, near), lax.rem(y + 2, NY)


def chunk(ref, zl):
    return ref[zl * EXPERTS:(zl + 1) * EXPERTS].reshape(ROWS, COLS)


def joined(first, second):
    return jnp.concatenate([first, second], axis=1)


def weights_in(w_in_ref, sib_ref, c, k):
    mine = w_in_ref[pl.ds(pl.multiple_of((k * NC + c) * COLS, COLS), COLS), :]
    return joined(mine, sib_ref[k])


def weights_out(w_out_ref, sib_ref, c, k):
    mine = w_out_ref[:, pl.ds(pl.multiple_of((k * NC + c) * COLS, COLS), COLS)]
    return jnp.concatenate([mine, sib_ref[k]], axis=0)


def forward(w_in_ref, w_out_ref, in_sib_ref, out_sib_ref, xs):
    _, c = position()
    at_of = places(position()[0], c)
    pre = jnp.zeros((ROWS, NC * HID), F32)
    act_grad = jnp.zeros((ROWS, NC * HID), F32)
    for place, blocks in xs:
        at = at_of[place] * NZ
        for zl in range(0, NZ, 2):
            x = joined(chunk(*blocks[zl]), chunk(*blocks[zl + 1]))
            w = jnp.concatenate([weights_in(w_in_ref, in_sib_ref, c, at + z) for z in (zl, zl + 1)], axis=0)
            v = joined(*[weights_out(w_out_ref, out_sib_ref, c, at + z) for z in (zl, zl + 1)])
            pre = pre + jnp.dot(x, w, preferred_element_type=F32)
            act_grad = act_grad + lax.dot_general(x, v, CONTRACT_LAST, preferred_element_type=F32)
    row = lax.broadcasted_iota(jnp.int32, (EXPERTS, MSG, NC * HID), 1).reshape(ROWS, NC * HID)
    return jnp.where(row < CAP, pre, act_grad)


def whole(ref):
    return [(ref, z) for z in range(NZ)]


def halves(low, high):
    return [(low, 0), (low, 1), (high, 0), (high, 1)]


def forward_first_kernel(wi, wo, wis, wos, own, first_a, first_b, out_ref):
    out_ref[...] = forward(wi, wo, wis, wos, [(0, whole(own)), (1, halves(first_a, first_b))])


def forward_second_kernel(wi, wo, wis, wos, second_a, second_b, before_ref, out_ref):
    out_ref[...] = before_ref[...] + forward(wi, wo, wis, wos, [(2, halves(second_a, second_b))])


def forward_last_kernel(wi, wo, wis, wos, last_a, last_b, before_ref, out_ref, sent_ref):
    total = before_ref[...] + forward(wi, wo, wis, wos, [(3, halves(last_a, last_b))])
    out_ref[...] = total
    sent_ref[...] = total.astype(BF16)


def activations(part_ref, part_sib_ref):
    passed = part_sib_ref[...]
    both = part_ref[...] + joined(passed[:, HID:], passed[:, :HID]).astype(F32)
    act_grad = jnp.concatenate([both[CAP:], both[:CAP]], axis=0)
    act, pullback = jax.vjp(lambda v: jax.nn.gelu(v, approximate=True), both)
    pre_grad = pullback(act_grad)[0]
    act = jnp.concatenate([act[ROWS - CAP:], act[:ROWS - CAP]], axis=0)
    row = lax.broadcasted_iota(jnp.int32, (EXPERTS, MSG, NC * HID), 1).reshape(ROWS, NC * HID)
    return jnp.where(row < CAP, pre_grad, 0.0).astype(BF16), jnp.where(row < CAP, 0.0, act).astype(BF16)


def partials(w_in_ref, sib_ref, pg, at, out_ref):
    _, c = position()
    for zl in range(0, NZ, 2):
        w = jnp.concatenate([weights_in(w_in_ref, sib_ref, c, at * NZ + z) for z in (zl, zl + 1)], axis=0)
        out = lax.dot_general(pg, w, CONTRACT_LAST, preferred_element_type=F32).astype(BF16)
        for j in range(2):
            out_ref[zl + j] = out[:, j * COLS:(j + 1) * COLS]


def far_kernel(w_in_ref, sib_ref, part_ref, part_sib_ref, pg_ref, out_ref):
    pre_grad, _ = activations(part_ref, part_sib_ref)
    pg = pre_grad.astype(F32).reshape(EXPERTS, MSG, NC * HID)[:, :CAP].reshape(KEPT, NC * HID).astype(BF16)
    pg_ref[...] = pg
    partials(w_in_ref, sib_ref, pg, places(*position())[3], out_ref)


def near_kernel(w_in_ref, sib_ref, pg_ref, *outs):
    pg = pg_ref[...]
    for at, out_ref in zip(places(*position()), outs):
        partials(w_in_ref, sib_ref, pg, at, out_ref)


def relay_kernel(mine_ref, passed_ref, out_ref):
    out_ref[...] = (mine_ref[...].astype(F32) + passed_ref[...].astype(F32)).astype(BF16)


def total_kernel(mine_ref, first_ref, second_ref, after_ref, out_ref):
    del after_ref
    out_ref[...] = (mine_ref[...].astype(F32) + first_ref[...].astype(F32) + second_ref[...].astype(F32)).astype(BF16)


def gathered_kernel(parts_ref, out_ref):
    total = parts_ref[0].astype(F32)
    for zl in range(1, NZ):
        total = total + parts_ref[zl].astype(F32)
    out_ref[...] = total.reshape(EXPERTS, CAP, COLS).astype(BF16)


def grads_kernel(part_ref, part_sib_ref, *refs):
    xs, (in_mine, out_mine, in_other, out_other) = refs[:7], refs[8:]
    left = joined(*activations(part_ref, part_sib_ref)).T
    xs = [whole(xs[0])] + [halves(*xs[i:i + 2]) for i in (1, 3, 5)]
    for y, blocks in zip(places(*position()), xs):
        at = y * NZ
        for zl in range(0, NZ, 2):
            x = joined(chunk(*blocks[zl]), chunk(*blocks[zl + 1]))
            both = jnp.dot(left, x, preferred_element_type=F32).astype(BF16)
            for ref, first in ((in_mine, 0), (in_other, HID)):
                turned = both[first:first + HID].T
                ref[at + zl] = turned[:COLS]
                ref[at + zl + 1] = turned[COLS:]
            lanes = pl.ds(pl.multiple_of((at + zl) * COLS, 2 * COLS), 2 * COLS)
            out_mine[:, lanes] = both[2 * HID:3 * HID]
            for j in range(2):
                out_other[at + zl + j] = both[3 * HID:, j * COLS:(j + 1) * COLS]


def merge_kernel(in_mine, out_mine, in_sib, out_sib, w_in_grad_ref, w_out_grad_ref):
    _, c = position()
    blocks = NY * NZ
    for k in range(blocks):
        mine = pl.ds(pl.multiple_of((k * NC + c) * COLS, COLS), COLS)
        other = pl.ds(pl.multiple_of((k * NC + 1 - c) * COLS, COLS), COLS)
        w_in_grad_ref[mine, :] = in_mine[k]
        w_in_grad_ref[other, :] = in_sib[k]
        w_out_grad_ref[:, mine] = out_mine[:, k * COLS:(k + 1) * COLS]
        w_out_grad_ref[:, other] = out_sib[k]


def combine_kernel(table_ref, back_ref, out_ref):
    rows = back_ref[...].astype(F32).reshape(KEPT, COLS).astype(BF16)
    out_ref[...] = jnp.dot(table_ref[...], rows, preferred_element_type=F32).astype(BF16)


SMEM = pl.BlockSpec(memory_space=pltpu.SMEM)
WHOLE = pl.BlockSpec(memory_space=pltpu.VMEM)
UNREAD = pl.BlockSpec(memory_space=pl.ANY)


def shape(*dims, kind=BF16):
    return jax.ShapeDtypeStruct(dims, kind)


def held(*dims, kind=BF16):
    return pltpu.VMEM(dims, kind)


def keep(value):
    return pltpu.with_memory_space_constraint(value, pltpu.VMEM)


def far(value):
    return pltpu.with_memory_space_constraint(value, pltpu.HBM)


def run(kernel, outs, scalars, *args, unread=0, scratch=()):
    specs = [SMEM] * scalars + [WHOLE] * (len(args) - scalars - unread) + [UNREAD] * unread
    out_specs = jax.tree.map(lambda _: WHOLE, outs)
    return pl.pallas_call(
        kernel, out_shape=outs, in_specs=specs, out_specs=out_specs, scratch_shapes=scratch, compiler_params=VMEM
    )(*args)


def partner(value, which):
    near, far = [i ^ 1 for i in range(NY)], [NY - 1 - i for i in range(NY)]
    to = [(near, far), (far, near)]
    return lax.ppermute(value, ("y", "c"), [(i * NC + c, to[c][which][i] * NC + c) for i in range(NY) for c in range(NC)])


def across(value):
    return lax.ppermute(value, "c", [(0, 1), (1, 0)])


def on_device(tokens, out_grad, expert_ids, gate_weights, w_in, w_out):
    ids, gate = far(expert_ids.T), far(gate_weights.T)
    w_in, w_out = w_in[0], w_out[0]
    blocks = NY * NZ
    half_in, half_out = held(blocks, COLS, HID), held(HID, blocks * COLS)
    send = run(dispatch_kernel, shape(EXPERTS, MSG, COLS), 0, ids, gate, far(tokens), far(out_grad))
    in_other, out_other = run(
        split_kernel, (half_in, half_in), 0, far(w_in.reshape(blocks, NC, COLS, HID)), far(w_out), send,
        unread=3, scratch=[pltpu.SemaphoreType.DMA((blocks + 1,))],
    )
    in_sib, out_sib = across(in_other), across(out_other)
    received = lax.all_to_all(send, ("zh", "x"), 0, 0, tiled=True)
    own = lax.all_gather(received, "zl", axis=0, tiled=True)
    own, in_sib, out_sib = lax.optimization_barrier((own, in_sib, out_sib))
    weights = (w_in, w_out, keep(in_sib), keep(out_sib))
    cut = NZ // 2 * EXPERTS
    low, high = own[:cut], own[cut:]
    first_a, second_b = partner(low, 0), partner(high, 1)
    first_b, second_a = partner(high, 0), partner(low, 1)
    last_a, last_b = partner(first_a, 1), partner(second_b, 0)
    xs = [keep(x) for x in (own, first_a, first_b, second_a, second_b, last_a, last_b)]
    part = held(ROWS, NC * HID, kind=F32)
    some = run(forward_first_kernel, part, 0, *weights, *xs[:3])
    more = run(forward_second_kernel, part, 0, *weights, *xs[3:5], keep(some))
    mine, sent = run(
        forward_last_kernel, (part, held(ROWS, NC * HID)), 0, *weights, *xs[5:], keep(more)
    )
    rows = held(NZ, KEPT, COLS)
    parts = keep(mine), keep(across(sent))
    pg, to_last = run(far_kernel, (held(KEPT, NC * HID), rows), 0, w_in, keep(in_sib), *parts)
    to_own, to_first, to_second = run(near_kernel, (rows, rows, rows), 0, w_in, keep(in_sib), keep(pg))
    passed, from_second = partner(to_last, 1), partner(to_second, 1)
    relayed = run(relay_kernel, rows, 0, keep(to_first), keep(passed))
    from_first = partner(relayed, 0)
    in_mine, out_mine, in_other, out_other = run(
        grads_kernel, (half_in, half_out, half_in, half_in), 0, *parts, *xs, relayed, unread=1
    )
    summed = run(total_kernel, rows, 0, keep(to_own), keep(from_first), keep(from_second), in_other, unread=1)
    collected = lax.all_to_all(summed, "zl", 0, 0, tiled=True)
    total = run(gathered_kernel, held(EXPERTS, CAP, COLS), 0, keep(collected))
    table = run(table_kernel, held(TOK, KEPT), 0, ids, total, unread=1)
    back = lax.all_to_all(total, ("zh", "x"), 0, 0, tiled=True)
    tokens_grad = run(combine_kernel, shape(TOK, COLS), 0, keep(table), keep(back))
    w_in_grad, w_out_grad = run(
        merge_kernel, (shape(*w_in.shape), shape(*w_out.shape)),
        0, keep(in_mine), keep(out_mine), keep(across(in_other)), keep(across(out_other)),
    )
    return tokens_grad, w_in_grad[None], w_out_grad[None]


def solution(mesh):
    fine = Mesh(mesh.devices.reshape(NY, NZ, NC, NH, NX), ("y", "zl", "c", "zh", "x"))
    dp, expert = ("y", "zl", "c"), ("zh", "x")
    placed = (
        P(expert, dp),
        P(expert, dp),
        P(expert, None),
        P(expert, None),
        P(expert, None, dp),
        P(expert, dp, None),
    )
    return jax.shard_map(
        on_device,
        mesh=fine,
        in_specs=placed,
        out_specs=(P(expert, dp), P(expert, None, dp), P(expert, dp, None)),
        check_vma=False,
    )
```
